32 devices in a mesh: image: 4 (over z), ri: 8 (over y, x, core).
Axes of the slice: x: 2, y: 2, z: 4, core: 2. Of those that a mesh axis runs over, the one named last changes fastest.
Arguments:
- blocks: bfloat16 [1024, 64, 256], P(('image', 'ri')), may hold values from -0.59765625 to 0.59765625
- block_owner: int32 [1024, 1], P(('image', 'ri')), may hold values from 0 to 7; in each aligned block of 32 rows (0 to 31, 32 to 63, ...) at most 8 rows name the same one
- block_basis: int32 [1024, 2], P(('image', 'ri')), may hold values from 0 to 255
- pair_images: int32 [1024, 2, 4], P(('image', 'ri')), may hold values from 0 to 3
- pair_cell: int32 [1024, 4], P(('image', 'ri')), may hold values from 0 to 3
- lattice: int32 [4, 2], replicated, may hold values from -3 to 3
- dens_occ: bfloat16 [4, 256, 64], P('image'), may hold values from -1.5 to 1.5
- dens_virt: bfloat16 [4, 256, 64], P('image'), may hold values from -1.5 to 1.5
Outputs:
- chi_k: float32 [2, 64, 8, 256, 256], P(None, None, 'ri', 'image')
The draws below stay inside these ranges and needn't reach their ends.
Inputs may be any that keep to these rules, and one draw needn't show every extreme that they name: `block_owner`: within the 32 blocks of one device no owner is named by more than 8 blocks.
All inputs are finite; a program needn't handle non-finite values.
Results may differ from the reference program's by a relative error of at most 0.0041.
Values may be sent and summed in bfloat16 or wider, within the bound.
No kernel may reach another device: no remote copies, remote signals or barrier semaphores. Data moves between devices by JAX's collectives and lax.ppermute only.
A program may use at most 128 MiB of HBM per device.

```python
import math
import jax
import jax.numpy as jnp
import numpy as np
from jax import lax

RI_DEV = 256
KK = 64
NBLK = 256
NIMG = 4
NLOC = 32
CAP = 8
NPAIR = 4
NCELL = 4
KGRID = 8
KPT = 64
BLOCKS = 1024
N_RI = 8


def with_ends(values, stream_key, least, top_value):
    index_at = [jax.random.randint(jax.random.fold_in(stream_key, axis), (), 0, length) for axis, length in enumerate(values.shape)]
    main_axis = values.shape.index(max(values.shape))
    next_to = index_at[:main_axis] + [(index_at[main_axis] + 1) % values.shape[main_axis]] + index_at[main_axis + 1:]
    return values.at[tuple(index_at)].set(least).at[tuple(next_to)].set(top_value)


def with_spikes(entries, rng, source, target, parts, factor):
    owner, partner = [(jnp.arange(entries.shape[dim]) // (entries.shape[dim] // parts)).reshape([-1 if axis == dim else 1 for axis in range(entries.ndim)]) for dim in (source, target)]
    chosen = jax.random.permutation(rng, parts)[partner]
    strong = (owner == chosen) | (owner == (partner + parts // 2) % parts)
    return jnp.where(strong, factor * entries, entries)


def levels(rng, dims, cuts, least, high):
    factor_of = 1.0
    for position, parts in cuts:
        draws = jax.random.uniform(jax.random.fold_in(jax.random.fold_in(rng, 6), position), (parts,), jnp.float32, least / len(cuts), high / len(cuts))
        factor_of = factor_of * jnp.repeat(jnp.exp(draws), dims[position] // parts).reshape((-1,) + (1,) * (len(dims) - 1 - position))
    return factor_of


def deal_out(own_key, own, number, rows, count, top, limit, skew):
    sequence = jax.random.permutation(own_key, count)
    packed, ordinary = portions_of(count, rows * top, limit, skew, True), portions_of(count, rows * top, limit, skew, False)
    places = jnp.arange(count)

    def named(tallies, rotation):
        used = int((tallies > 0).sum())
        fixed = max(1, used // 4)
        shifted = fixed + (places - fixed + rotation * (used - fixed)) % max(1, count - fixed)
        return jnp.zeros((count,), jnp.int32).at[sequence[jnp.where(places < fixed, places, shifted)]].set(jnp.asarray(tallies, jnp.int32))

    tallies = jnp.where(number % 4 == 0, named(packed, number // 4), named(ordinary, number - number // 4 - 1))
    mixed = jax.random.permutation(jax.random.fold_in(own, 3), count)
    donor, taker = mixed[0:count // 2 * 2:2], mixed[1:count // 2 * 2:2]
    slack = jnp.minimum(tallies[donor] - 1, limit - tallies[taker]) // 2
    slack = jnp.where((donor == sequence[0]) | (taker == sequence[0]) | (tallies[taker] == 0), 0, jnp.maximum(slack, 0))
    shifted = jax.random.randint(jax.random.fold_in(own, 4), (count // 2,), 0, 1 << 20) % (slack + 1)
    tallies = tallies.at[donor].add(-shifted).at[taker].add(shifted)
    members = jnp.searchsorted(jnp.cumsum(tallies), jnp.arange(rows * top), side="right").astype(jnp.int32)
    table = members.reshape(top, rows).T
    table = table[jax.random.permutation(jax.random.fold_in(own, 1), rows)]
    rotation = jax.random.randint(jax.random.fold_in(own, 2), (rows, 1), 0, top)
    return jnp.take_along_axis(table, (jnp.arange(top)[None, :] + rotation) % top, axis=1)


def portions_of(amount, total, reach, lean, full):
    weights = [(1 << 20) // math.isqrt(grade ** lean) + 1 for grade in range(1, amount + 1)]
    largest = reach if full else min(reach, max(-(-total // amount), total * weights[0] // sum(weights)))
    least = 1 if total - largest >= amount - 1 else 0
    given, rest = [largest] + [least] * (amount - 1), total - largest - least * (amount - 1)
    while rest > 0:
        candidates = [i for i in range(1, amount) if given[i] < largest] or [i for i in range(1, amount) if given[i] < reach]
        pool, remaining = sum([weights[i] for i in candidates]), rest
        for i in candidates:
            extra = min(reach - given[i], max(1, remaining * weights[i] // pool), rest)
            given[i] = given[i] + extra
            rest = rest - extra
    return np.array(given)


def normal_values(stream_key, shape, scale, bound, cuts=(), held_as=jnp.bfloat16):
    values = jax.random.normal(stream_key, shape, jnp.float32) * scale
    if len(cuts) > 0:
        values = levels(stream_key, shape, cuts, -0.22, 0.18) * values
    return jnp.clip(values, min=-bound, max=bound).astype(held_as)


def gaussian_with(key, shape, spread, reach, cuts, heavy, held_as=jnp.bfloat16):
    drawn = spread * jax.random.normal(key, shape, jnp.float32)
    if cuts:
        drawn = drawn * levels(key, shape, cuts, -0.22, 0.18)
    return jnp.clip(with_spikes(drawn, jax.random.fold_in(key, 3), *heavy), -reach, reach).astype(held_as)


def setup_inputs(seed: int = 0) -> dict:
    key_list = jax.random.split(jax.random.key(seed), 9)
    blocks = gaussian_with(key_list[0], (BLOCKS, KK, RI_DEV), 0.1, 0.59765625, ((0, 32),), (0, 2, 32, 2.75))
    block_owner_keys = jax.random.split(jax.random.fold_in(key_list[1], 1), BLOCKS // NLOC)
    block_owner_turns = jax.random.permutation(jax.random.fold_in(key_list[1], 3), BLOCKS // NLOC)
    block_owner = jax.vmap(lambda own, number: deal_out(jax.random.fold_in(key_list[1], 2), own, number, NLOC, N_RI, 1, CAP, 2))(block_owner_keys, block_owner_turns).reshape((BLOCKS, 1))
    block_basis = with_ends(jax.random.randint(key_list[2], (BLOCKS, 2), 0, NBLK), jax.random.fold_in(key_list[2], 1), 0, NBLK - 1).astype(jnp.int32)
    pair_images = with_ends(jax.random.randint(key_list[3], (BLOCKS, 2, NPAIR), 0, NIMG), jax.random.fold_in(key_list[3], 1), 0, NIMG - 1).astype(jnp.int32)
    pair_cell = with_ends(jax.random.randint(key_list[4], (BLOCKS, NPAIR), 0, NCELL), jax.random.fold_in(key_list[4], 1), 0, NCELL - 1).astype(jnp.int32)
    lattice = with_ends(jax.random.randint(key_list[5], (NCELL, 2), -3, 4), jax.random.fold_in(key_list[5], 1), -3, 3).astype(jnp.int32)
    dens_occ = normal_values(key_list[6], (NIMG, NBLK, KK), 0.25, 1.5, ((0, 4),))
    dens_virt = normal_values(key_list[7], (NIMG, NBLK, KK), 0.25, 1.5, ((0, 4),))
    return dict(blocks=blocks, block_owner=block_owner, block_basis=block_basis, pair_images=pair_images, pair_cell=pair_cell, lattice=lattice, dens_occ=dens_occ, dens_virt=dens_virt)


def density_terms(running, occ_piece, first_image, virt_whole, listing, pair_count, cell_count):
    image_count, block_count, square = occ_piece.shape
    side_len = math.isqrt(square)
    row_count = listing.shape[0]
    first_block = listing[:, 0]
    second = listing[:, 1]
    occ_img = listing[:, 2:2 + pair_count]
    virt_img = listing[:, 2 + pair_count:2 + 2 * pair_count]
    cell_ids = listing[:, 2 + 2 * pair_count:2 + 3 * pair_count]
    offset = occ_img - first_image
    inside = ((offset >= 0) & (offset < image_count)).astype(jnp.float32)
    occ_rows = (jnp.clip(offset, 0, image_count - 1) * block_count + first_block[:, None]).astype(jnp.int32)
    virt_rows = (virt_img * block_count + second[:, None]).astype(jnp.int32)
    occ_vals = occ_piece.reshape(image_count * block_count, square)[occ_rows].astype(jnp.float32) * inside[:, :, None]
    virt_vals = virt_whole.reshape(-1, square)[virt_rows].astype(jnp.float32)
    select = (cell_ids[:, :, None] == jnp.arange(cell_count, dtype=jnp.int32)[None, None, :]).astype(jnp.float32)
    term_sum = jnp.einsum('sjr,sjlm,sjnq->srlqmn', select, occ_vals.reshape(row_count, pair_count, side_len, side_len), virt_vals.reshape(row_count, pair_count, side_len, side_len), precision=lax.Precision.HIGHEST)
    return running + term_sum.reshape(row_count, cell_count, square, square)

def reference(blocks, block_owner, block_basis, pair_images, pair_cell, lattice, dens_occ, dens_virt):
    listing = jnp.concatenate([block_basis, pair_images[:, 0, :], pair_images[:, 1, :], pair_cell], axis=1).astype(jnp.int32)
    batch_count = BLOCKS // NLOC

    def per_batch(chi_all, pieces):
        blk_part, list_part, own_part = pieces
        zero_ops = jnp.zeros((NLOC, NCELL, KK, KK), jnp.float32)
        density_ops = density_terms(zero_ops, dens_occ, 0, dens_virt, list_part, NPAIR, NCELL).astype(jnp.bfloat16)
        mixed_rows = jnp.einsum('srkm,smp->srkp', density_ops.astype(jnp.float32), blk_part.astype(jnp.float32), precision=lax.Precision.HIGHEST).astype(jnp.bfloat16)
        contrib = jnp.einsum('srkp,skq->srpq', mixed_rows.astype(jnp.float32), blk_part.astype(jnp.float32), precision=lax.Precision.HIGHEST)
        return (chi_all.at[own_part].add(contrib), None)
    chi_start = jnp.zeros((N_RI, NCELL, RI_DEV, RI_DEV), jnp.float32)
    chi_cells, _ = lax.scan(per_batch, chi_start, (blocks.reshape(batch_count, NLOC, KK, RI_DEV), listing.reshape(batch_count, NLOC, -1), block_owner[:, 0].astype(jnp.int32).reshape(batch_count, NLOC)))
    points = jnp.arange(KPT, dtype=jnp.int32)
    wrapped = ((points // KGRID)[:, None] * lattice[None, :, 0] + (points % KGRID)[:, None] * lattice[None, :, 1]) % KGRID
    angles = 2.0 * math.pi / KGRID * wrapped.astype(jnp.float32)
    phases = jnp.concatenate([jnp.cos(angles), jnp.sin(angles)], axis=0)
    result = jnp.einsum('cr,orpq->copq', phases, chi_cells, precision=lax.Precision.HIGHEST)
    return result.reshape(2, KPT, N_RI, RI_DEV, RI_DEV)
```

```python
import functools
import math

import jax
import jax.numpy as jnp
from jax import lax
from jax.experimental import pallas as pl
from jax.experimental.pallas import tpu as pltpu
from jax.sharding import PartitionSpec as P

KGRID = 8
QUAD = 4
LIST_ROWS = 16
BF16 = jnp.bfloat16
F32 = jnp.float32
VMEM_LIMIT = 48 * 1024 * 1024


def iota(shape, dim):
    return lax.broadcasted_iota(jnp.int32, shape, dim)


def pack_kernel(
    n, cap, pairs, owner_s, owner_v, basis, images, cells, blocks, *rest
):
    outs, (nothing, table, lists, count, place, sems, list_sems) = rest[:n], rest[n:]
    rows, square, width = blocks.shape
    me = lax.axis_index("ri")
    nothing[...] = jnp.zeros_like(nothing)
    for k in range(n):
        count[k] = 0

    @pl.loop(0, rows)
    def _(e):
        k = owner_s[0, e] ^ me
        r = count[k]
        place[k * cap + r] = e
        count[k] = r + 1

    def slot(k, r, source):
        return pltpu.make_async_copy(
            source, outs[k].at[pl.ds(r * square, square)], sems.at[k * cap + r]
        )

    for k in range(n):
        for r in range(cap):
            used = r < count[k]

            @pl.when(used)
            def _():
                slot(k, r, blocks.at[place[k * cap + r]]).start()

            @pl.when(jnp.logical_not(used))
            def _():
                slot(k, r, nothing).start()

    distance = owner_v[...] ^ me
    as_column = jnp.sum(
        jnp.where(iota((rows, rows), 0) == iota((rows, rows), 1), distance, 0),
        axis=1,
        keepdims=True,
    )
    before = (as_column == distance) & (iota((rows, rows), 0) < iota((rows, rows), 1))
    rank = jnp.sum(before.astype(jnp.int32), axis=0, keepdims=True)
    chosen = iota((n * LIST_ROWS, rows), 0) == distance * LIST_ROWS + rank
    table[...] = jnp.zeros_like(table)
    table[0:2, :] = basis[...].astype(F32)
    table[2 : 2 + pairs, :] = images[0].astype(F32)
    table[2 + pairs : 2 + 2 * pairs, :] = images[1].astype(F32)
    table[2 + 2 * pairs : 2 + 3 * pairs, :] = cells[...].astype(F32)
    ordered = lax.dot_general(
        chosen.astype(BF16),
        table[...].astype(BF16),
        (((1,), (1,)), ((), ())),
        preferred_element_type=F32,
    )
    lists[:, 0:128] = ordered.astype(BF16)
    lists[:, 128:width] = jnp.zeros((n * LIST_ROWS, width - 128), BF16)

    def list_copy(k):
        return pltpu.make_async_copy(
            lists.at[pl.ds(k * LIST_ROWS, LIST_ROWS)],
            outs[k].at[pl.ds(cap * square, LIST_ROWS)],
            list_sems.at[k],
        )

    for k in range(n):
        list_copy(k).start()
    for k in range(n):
        for r in range(cap):
            slot(k, r, nothing).wait()
        list_copy(k).wait()


def pack(n, cap, blocks, block_owner, block_basis, pair_images, pair_cell):
    rows, square, width = blocks.shape
    pairs = pair_cell.shape[1]
    owner = block_owner.T
    vmem = pl.BlockSpec(memory_space=pltpu.VMEM)
    payload = jax.ShapeDtypeStruct((cap * square + LIST_ROWS, width), BF16)
    return pl.pallas_call(
        functools.partial(pack_kernel, n, cap, pairs),
        out_shape=[payload] * n,
        in_specs=[pl.BlockSpec(memory_space=pltpu.SMEM), vmem, vmem, vmem, vmem]
        + [pl.BlockSpec(memory_space=pl.ANY)],
        out_specs=[pl.BlockSpec(memory_space=pl.ANY)] * n,
        scratch_shapes=[
            pltpu.VMEM((square, width), BF16),
            pltpu.VMEM((128, rows), F32),
            pltpu.VMEM((n * LIST_ROWS, width), BF16),
            pltpu.SMEM((n,), jnp.int32),
            pltpu.SMEM((n * cap,), jnp.int32),
            pltpu.SemaphoreType.DMA((n * cap,)),
            pltpu.SemaphoreType.DMA((n,)),
        ],
        compiler_params=pltpu.CompilerParams(vmem_limit_bytes=VMEM_LIMIT),
        cost_estimate=pl.CostEstimate(flops=0, bytes_accessed=6 << 20, transcendentals=0),
        name="pack_by_owner",
    )(
        owner,
        owner,
        block_basis.T,
        jnp.transpose(pair_images, (1, 2, 0)),
        pair_cell.T,
        blocks,
    )


def dot(a, b, contract=(1, 0)):
    return lax.dot_general(
        a, b, (((contract[0],), (contract[1],)), ((), ())), preferred_element_type=F32
    )


def chi_kernel(cap, pairs, cell_count, first, last, *refs):
    refs = list(refs)
    images = lax.axis_size("image")
    payloads = [refs.pop(0) for _ in range(QUAD)]
    pieces = [refs.pop(0) for _ in range(images)]
    before = None if first else refs.pop(0)
    if last:
        own, *sends = [refs.pop(0) for _ in range(images)]
        total = refs.pop(0)
    else:
        total = refs.pop(0)
    mixed, stacked = refs
    z = lax.axis_index("image")
    width = payloads[0].shape[1]
    square = (payloads[0].shape[0] - LIST_ROWS) // cap
    side = math.isqrt(square)
    lanes = QUAD * square
    list_at = cap * square

    lane = iota((1, lanes), 1)
    listing = jnp.concatenate(
        [p[list_at : list_at + LIST_ROWS, 0:128].astype(F32)[0:8] for p in payloads], axis=0
    )

    def columns(start):
        return jnp.concatenate(
            [listing[:, start + j : start + j + 1] for j in range(pairs)], axis=0
        ).astype(jnp.int32)

    def to_lanes(rows):
        out = []
        for j in range(pairs):
            acc = 0.0
            for s in range(QUAD):
                at = (j * QUAD + s) * 8
                acc = acc + jnp.where(lane // square == s, rows[at : at + 8], 0.0)
            out.append(acc)
        return out

    def density_rows(basis_at, image_at, piece_at):
        block = jnp.concatenate([listing[:, basis_at : basis_at + 1]] * pairs, axis=0)
        block = block.astype(jnp.int32)
        image = columns(image_at) ^ z
        block_count = pieces[0].shape[1]
        hit = iota((QUAD * 8 * pairs, block_count), 1) == block
        found = 0.0
        for i in range(images):
            part = pieces[i][piece_at : piece_at + square, :]
            chosen = jnp.where(hit & (image == i), 1.0, 0.0).astype(BF16)
            found = found + dot(chosen, jnp.concatenate([part] * QUAD, axis=0), (1, 1))
        return to_lanes(found)

    occ = density_rows(0, 2, 0)
    virt = density_rows(1, 2 + pairs, square)
    cell = to_lanes(columns(2 + 2 * pairs).astype(F32))

    shape = (square, lanes)
    occ_mask = (iota(shape, 1) % side == iota(shape, 0) // side).astype(BF16)
    virt_mask = (iota(shape, 1) % square // side == iota(shape, 0) % side).astype(BF16)
    shape = (lanes, lanes)
    occ_spread = (iota(shape, 0) // side == iota(shape, 1) // side).astype(BF16)
    virt_spread = (
        (iota(shape, 0) // square == iota(shape, 1) // square)
        & (iota(shape, 0) % side == iota(shape, 1) % side)
    ).astype(BF16)
    own_lanes = [(lane // square == s) for s in range(QUAD)]

    for r in range(cap):
        rows = slice(r * square, (r + 1) * square)
        block = jnp.concatenate([p[rows, :] for p in payloads], axis=0)
        stacked[r * lanes : (r + 1) * lanes, :] = block
        turned = block.T
        occ_in = jnp.concatenate([occ_mask * o[r : r + 1].astype(BF16) for o in occ], axis=0)
        virt_in = jnp.concatenate([virt_mask * v[r : r + 1].astype(BF16) for v in virt], axis=0)
        terms = dot(occ_in, occ_spread) * dot(virt_in, virt_spread)
        for c in range(cell_count):
            op = 0.0
            for j in range(pairs):
                here = cell[j][r : r + 1] == float(c)
                op = op + jnp.where(here, terms[j * square : (j + 1) * square], 0.0)
            diagonal = jnp.concatenate([jnp.where(m, op, 0.0) for m in own_lanes], axis=0)
            mixed[c, :, r * lanes : (r + 1) * lanes] = dot(turned, diagonal.astype(BF16)).astype(
                BF16
            )
    for c in range(cell_count):
        acc = dot(mixed[c], stacked[...])
        if not first:
            acc = acc + before[c]
        total[c] = acc
    if last:
        share = own.shape[1]
        own[...] = total[:, pl.ds(pl.multiple_of(z * share, share), share), :]
        for k in range(1, images):
            at = pl.multiple_of((z ^ k) * share, share)
            sends[k - 1][...] = total[:, pl.ds(at, share), :].astype(BF16)


def chi_part(cap, pairs, cell_count, payloads, pieces, before, last):
    images = len(pieces)
    width = payloads[0].shape[1]
    square = (payloads[0].shape[0] - LIST_ROWS) // cap
    vmem = pl.BlockSpec(memory_space=pltpu.VMEM)
    full = jax.ShapeDtypeStruct((cell_count, width, width), F32)
    share = (cell_count, width // images, width)
    args = list(payloads) + list(pieces) + ([] if before is None else [before])
    scratch = [
        pltpu.VMEM((cell_count, width, cap * QUAD * square), BF16),
        pltpu.VMEM((cap * QUAD * square, width), BF16),
    ]
    if last:
        out_shape = [jax.ShapeDtypeStruct(share, F32)] + [jax.ShapeDtypeStruct(share, BF16)] * (
            images - 1
        )
        scratch = [pltpu.VMEM(full.shape, F32)] + scratch
    else:
        out_shape = [full]
    return pl.pallas_call(
        functools.partial(chi_kernel, cap, pairs, cell_count, before is None, last),
        out_shape=out_shape,
        in_specs=[vmem] * len(args),
        out_specs=[vmem] * len(out_shape),
        scratch_shapes=scratch,
        compiler_params=pltpu.CompilerParams(vmem_limit_bytes=VMEM_LIMIT),
        cost_estimate=pl.CostEstimate(
            flops=2 * cap * QUAD * 3 * square * cell_count * width * width // 2,
            bytes_accessed=4 << 20,
            transcendentals=0,
        ),
        name="chi_of_payloads",
    )(*args)


def transform_kernel(cell_count, phases, own, *rest):
    *received, out, total = rest

    @pl.when(pl.program_id(0) == 0)
    def _():
        acc = own[...]
        for part in received:
            acc = acc + part[...].astype(F32)
        total[...] = acc

    points = out.shape[0]
    base = pl.program_id(0) * points
    for row in range(0, out.shape[1], 8):
        parts = [total[c, row : row + 8, :] for c in range(cell_count)]
        for i in range(points):
            acc = phases[base + i, 0] * parts[0]
            for c in range(1, cell_count):
                acc = acc + phases[base + i, c] * parts[c]
            out[i, row : row + 8, :] = acc


def transform(phases, own, received):
    cell_count, share, width = own.shape
    points = phases.shape[0]
    step = 8
    whole = pl.BlockSpec((cell_count, share, width), lambda i: (0, 0, 0))
    return pl.pallas_call(
        functools.partial(transform_kernel, cell_count),
        grid=(points // step,),
        out_shape=jax.ShapeDtypeStruct((points, share, width), F32),
        in_specs=[pl.BlockSpec(memory_space=pltpu.SMEM)] + [whole] * (1 + len(received)),
        out_specs=pl.BlockSpec((step, share, width), lambda i: (i, 0, 0)),
        scratch_shapes=[pltpu.VMEM((cell_count, share, width), F32)],
        compiler_params=pltpu.CompilerParams(vmem_limit_bytes=VMEM_LIMIT),
        cost_estimate=pl.CostEstimate(
            flops=2 * points * cell_count * share * width,
            bytes_accessed=points * share * width * 4,
            transcendentals=0,
        ),
        name="to_k_points",
    )(phases, own, *received)


def swap(array, axis, k):
    size = lax.axis_size(axis)
    return lax.ppermute(array, axis, [(i, i ^ k) for i in range(size)])


def local(blocks, block_owner, block_basis, pair_images, pair_cell, lattice, dens_occ, dens_virt):
    owners, images = lax.axis_size("ri"), lax.axis_size("image")
    pairs = pair_cell.shape[1]
    cell_count = lattice.shape[0]
    cap = max(2, (2 * blocks.shape[0] + owners - 1) // owners)

    packed = pack(owners, cap, blocks, block_owner, block_basis, pair_images, pair_cell)
    density = jnp.concatenate([dens_occ[0].T, dens_virt[0].T], axis=0)
    pieces = [density] + [swap(density, "image", k) for k in range(1, images)]
    payloads = [packed[0]] + [swap(packed[k], "ri", k) for k in range(1, owners)]

    chi = None
    for at in range(0, owners, QUAD):
        last = at + QUAD >= owners
        out = chi_part(cap, pairs, cell_count, payloads[at : at + QUAD], pieces, chi, last)
        chi = out[0]
    own, sends = out[0], out[1:]
    received = [swap(sends[k - 1], "image", k) for k in range(1, images)]

    points = jnp.arange(KGRID * KGRID, dtype=jnp.int32)
    wrapped = (
        (points // KGRID)[:, None] * lattice[None, :, 0]
        + (points % KGRID)[:, None] * lattice[None, :, 1]
    ) % KGRID
    angles = 2.0 * math.pi / KGRID * wrapped.astype(F32)
    phases = jnp.concatenate([jnp.cos(angles), jnp.sin(angles)], axis=0)
    result = transform(phases, own, received)
    return result.reshape(2, KGRID * KGRID, 1, own.shape[1], own.shape[2])


def solution(mesh):
    placed = (
        P(("image", "ri"), None, None),
        P(("image", "ri"), None),
        P(("image", "ri"), None),
        P(("image", "ri"), None, None),
        P(("image", "ri"), None),
        P(),
        P("image", None, None),
        P("image", None, None),
    )
    return jax.shard_map(
        local,
        mesh=mesh,
        in_specs=placed,
        out_specs=P(None, None, "ri", "image", None),
        check_vma=False,
    )
```

```python
import functools
import math

import jax
import jax.numpy as jnp
from jax import lax
from jax.experimental import pallas as pl
from jax.experimental.pallas import tpu as pltpu
from jax.sharding import PartitionSpec as P

KGRID = 8
PART = 5
QUAD = 4
LIST_ROWS = 16
BF16 = jnp.bfloat16
F32 = jnp.float32
VMEM_LIMIT = 48 * 1024 * 1024
CHI_FLOPS, CHI_BYTES = 1 << 20, 1 << 10
PACK_LIMIT = 48 * 1024 * 1024


def iota(shape, dim):
    return lax.broadcasted_iota(jnp.int32, shape, dim)


def dot(a, b, contract=(1, 0)):
    return lax.dot_general(
        a, b, (((contract[0],), (contract[1],)), ((), ())), preferred_element_type=F32
    )


def pack_kernel(n, cap, pairs, *refs):
    ints, from_blocks, outs, rest = refs[0], refs[1], refs[2 : 2 + n], refs[2 + n :]
    owner, blocks, table, lists, count, place, sems = rest
    rows, square, width = blocks.shape
    me = lax.axis_index("ri")
    pieces = 4
    part = rows // pieces
    started = [pltpu.make_async_copy(ints.at[pl.ds(0, 8)], owner, sems.at[pieces])]
    for i in range(pieces):
        at = pl.ds(i * part, part)
        started.append(pltpu.make_async_copy(from_blocks.at[at], blocks.at[at], sems.at[i]))
    for copy in started:
        copy.start()
    for k in range(n):
        count[k] = 0
    for k in range(n * cap):
        place[k] = 0
    table[...] = jnp.zeros_like(table)
    lists[...] = jnp.zeros_like(lists)

    distance = ints[0:1, :] ^ me
    as_column = jnp.sum(
        jnp.where(iota((rows, rows), 0) == iota((rows, rows), 1), distance, 0),
        axis=1,
        keepdims=True,
    )
    before = (as_column == distance) & (iota((rows, rows), 0) < iota((rows, rows), 1))
    rank = jnp.sum(before.astype(jnp.int32), axis=0, keepdims=True)
    chosen = iota((n * LIST_ROWS, rows), 0) == distance * LIST_ROWS + rank
    table[0 : ints.shape[0], :] = ints[...].astype(F32)
    table[ints.shape[0] - pairs : ints.shape[0], :] += 1.0
    ordered = dot(chosen.astype(BF16), table[...].astype(BF16), (1, 1))
    lists[:, 0:128] = ordered.astype(BF16)

    started[0].wait()

    @pl.loop(0, rows, unroll=4)
    def _(e):
        k = owner[0, e] ^ me
        r = count[k]
        place[k * cap + r] = e
        count[k] = r + 1

    for copy in started[1:]:
        copy.wait()
    for k in range(n):
        for r in range(cap):
            outs[k][r * square : (r + 1) * square, :] = blocks[place[k * cap + r]]
        outs[k][cap * square :, :] = lists[k * LIST_ROWS : (k + 1) * LIST_ROWS, :]


def pack(n, cap, blocks, block_owner, block_basis, pair_images, pair_cell):
    rows, square, width = blocks.shape
    pairs = pair_cell.shape[1]
    ints = jnp.concatenate(
        [
            block_owner.T,
            block_basis.T,
            jnp.transpose(pair_images, (1, 2, 0)).reshape(2 * pairs, rows),
            pair_cell.T,
        ],
        axis=0,
    )
    payload = jax.ShapeDtypeStruct((cap * square + LIST_ROWS, width), BF16)
    return pl.pallas_call(
        functools.partial(pack_kernel, n, cap, pairs),
        out_shape=[payload] * n,
        in_specs=[
            pl.BlockSpec(memory_space=pltpu.VMEM),
            pl.BlockSpec(memory_space=pltpu.HBM),
        ],
        out_specs=[pl.BlockSpec(memory_space=pltpu.VMEM)] * n,
        scratch_shapes=[
            pltpu.SMEM((8, rows), jnp.int32),
            pltpu.VMEM(blocks.shape, BF16),
            pltpu.VMEM((128, rows), F32),
            pltpu.VMEM((n * LIST_ROWS, width), BF16),
            pltpu.SMEM((n,), jnp.int32),
            pltpu.SMEM((n * cap,), jnp.int32),
            pltpu.SemaphoreType.DMA((5,)),
        ],
        compiler_params=pltpu.CompilerParams(vmem_limit_bytes=PACK_LIMIT),
        cost_estimate=pl.CostEstimate(flops=0, bytes_accessed=6 << 20, transcendentals=0),
        name="pack_by_owner",
    )(ints, blocks)


def chi_kernel(count, cap, pairs, cell_count, first, last, *refs):
    refs = list(refs)
    images = lax.axis_size("image")
    payloads = [refs.pop(0) for _ in range(count)]
    pieces = [refs.pop(0) for _ in range(images)]
    before = None if first else refs.pop(0)
    if last:
        own, *sends = [refs.pop(0) for _ in range(images)]
    total = refs.pop(0)
    mixed, stacked = refs
    z = lax.axis_index("image")
    square = (payloads[0].shape[0] - LIST_ROWS) // cap
    side = math.isqrt(square)
    quad = min(QUAD, cap)
    lanes = quad * square
    list_at = cap * square

    lane = iota((1, lanes), 1)
    listing = jnp.concatenate(
        [p[list_at : list_at + LIST_ROWS, 0:128].astype(F32)[0:8] for p in payloads], axis=0
    )
    height = 8 * count

    def columns(start):
        return jnp.concatenate(
            [listing[:, start + j : start + j + 1] for j in range(pairs)], axis=0
        ).astype(jnp.int32)

    def side_by_side(rows, at):
        out = jnp.where(lane // square == 0, rows[at : at + 1], 0.0)
        for s in range(1, quad):
            out = jnp.where(lane // square == s, rows[at + s : at + s + 1], out)
        return out

    def density_rows(basis_at, image_at, piece_at):
        block = jnp.concatenate([listing[:, basis_at : basis_at + 1]] * pairs, axis=0)
        block = block.astype(jnp.int32)
        image = columns(image_at) ^ z
        block_count = pieces[0].shape[1]
        hit = iota((height * pairs, block_count), 1) == block
        found = 0.0
        for i in range(images):
            part = pieces[i][piece_at : piece_at + square, :]
            chosen = jnp.where(hit & (image == i), 1.0, 0.0).astype(BF16)
            found = found + dot(chosen, jnp.concatenate([part] * quad, axis=0), (1, 1))
        return found

    occ = density_rows(1, 3, 0)
    virt = density_rows(2, 3 + pairs, square)
    cell = jnp.broadcast_to(columns(3 + 2 * pairs).astype(F32), (height * pairs, lanes))

    shape = (square, lanes)
    occ_mask = (iota(shape, 1) % side == iota(shape, 0) // side).astype(BF16)
    virt_mask = (iota(shape, 1) % square // side == iota(shape, 0) % side).astype(BF16)
    shape = (lanes, lanes)
    occ_spread = (iota(shape, 0) // side == iota(shape, 1) // side).astype(BF16)
    virt_spread = (
        (iota(shape, 0) // square == iota(shape, 1) // square)
        & (iota(shape, 0) % side == iota(shape, 1) % side)
    ).astype(BF16)

    groups = [(p, g) for p in range(count) for g in range(cap // quad)]
    for i, (p, g) in enumerate(groups):
        block = payloads[p][g * lanes : (g + 1) * lanes, :]
        stacked[i * lanes : (i + 1) * lanes, :] = block
        turned = block.T
        at = [j * height + 8 * p + g * quad for j in range(pairs)]
        occ_in = jnp.concatenate(
            [occ_mask * side_by_side(occ, a).astype(BF16) for a in at], axis=0
        )
        virt_in = jnp.concatenate(
            [virt_mask * side_by_side(virt, a).astype(BF16) for a in at], axis=0
        )
        terms = dot(occ_in, occ_spread) * dot(virt_in, virt_spread)
        here = [side_by_side(cell, a) for a in at]
        for c in range(cell_count):
            op = 0.0
            for j in range(pairs):
                term = terms[j * square : (j + 1) * square]
                op = op + jnp.where(here[j] == float(c + 1), term, 0.0)
            diagonal = jnp.concatenate(
                [jnp.where(lane // square == s, op, 0.0) for s in range(quad)], axis=0
            )
            mixed[c, :, i * lanes : (i + 1) * lanes] = dot(turned, diagonal.astype(BF16)).astype(
                BF16
            )
    for c in range(cell_count):
        acc = dot(mixed[c], stacked[...])
        if not first:
            acc = acc + before[c]
        total[c] = acc
    if last:
        share = own.shape[1]
        own[...] = total[:, pl.ds(pl.multiple_of(z * share, share), share), :]
        for k in range(1, images):
            at = pl.multiple_of((z ^ k) * share, share)
            sends[k - 1][...] = total[:, pl.ds(at, share), :].astype(BF16)


def chi_part(cap, pairs, cell_count, payloads, pieces, before, last):
    images, count = len(pieces), len(payloads)
    width = payloads[0].shape[1]
    square = (payloads[0].shape[0] - LIST_ROWS) // cap
    depth = count * cap * square
    vmem = pl.BlockSpec(memory_space=pltpu.VMEM)
    full = jax.ShapeDtypeStruct((cell_count, width, width), F32)
    share = (cell_count, width // images, width)
    args = list(payloads) + list(pieces) + ([] if before is None else [before])
    scratch = [pltpu.VMEM((cell_count, width, depth), BF16), pltpu.VMEM((depth, width), BF16)]
    if last:
        out_shape = [jax.ShapeDtypeStruct(share, F32)] + [jax.ShapeDtypeStruct(share, BF16)] * (
            images - 1
        )
        scratch = [pltpu.VMEM(full.shape, F32)] + scratch
    else:
        out_shape = [full]
    return pl.pallas_call(
        functools.partial(chi_kernel, count, cap, pairs, cell_count, before is None, last),
        out_shape=out_shape,
        in_specs=[vmem] * len(args),
        out_specs=[vmem] * len(out_shape),
        scratch_shapes=scratch,
        compiler_params=pltpu.CompilerParams(vmem_limit_bytes=VMEM_LIMIT),
        cost_estimate=pl.CostEstimate(
            flops=CHI_FLOPS, bytes_accessed=CHI_BYTES, transcendentals=0
        ),
        name="chi_of_payloads",
    )(*args)


def transform_kernel(cell_count, step, phases, own, *rest):
    *received, out, total, shaped, sems = rest
    acc = own[...]
    for part in received:
        acc = acc + part[...].astype(F32)
    total[...] = acc
    points, share, width = out.shape
    tile = min(share, 32)

    def copy(i):
        at = pl.ds(i * step, step)
        return pltpu.make_async_copy(shaped.at[at], out.at[at], sems.at[i])

    @pl.loop(0, points // step)
    def _(i):
        for row in range(0, share, tile):
            parts = [total[c, row : row + tile, :] for c in range(cell_count)]
            for j in range(step):
                acc = phases[0, i * step + j] * parts[0]
                for c in range(1, cell_count):
                    acc = acc + phases[c, i * step + j] * parts[c]
                shaped[i * step + j, row : row + tile, :] = acc
        copy(i).start()

    @pl.loop(0, points // step)
    def _(i):
        copy(i).wait()


def transform(phases, own, received):
    cell_count, share, width = own.shape
    points = phases.shape[1]
    step = 8
    vmem = pl.BlockSpec(memory_space=pltpu.VMEM)
    return pl.pallas_call(
        functools.partial(transform_kernel, cell_count, step),
        out_shape=jax.ShapeDtypeStruct((points, share, width), F32),
        in_specs=[pl.BlockSpec(memory_space=pltpu.SMEM)] + [vmem] * (1 + len(received)),
        out_specs=pl.BlockSpec(memory_space=pltpu.HBM),
        scratch_shapes=[
            pltpu.VMEM((cell_count, share, width), F32),
            pltpu.VMEM((points, share, width), F32),
            pltpu.SemaphoreType.DMA((points // step,)),
        ],
        compiler_params=pltpu.CompilerParams(vmem_limit_bytes=VMEM_LIMIT),
        cost_estimate=pl.CostEstimate(
            flops=2 * points * cell_count * share * width,
            bytes_accessed=points * share * width * 4,
            transcendentals=0,
        ),
        name="to_k_points",
    )(phases, own, *received)


def swap(array, axis, k):
    size = lax.axis_size(axis)
    return lax.ppermute(array, axis, [(i, i ^ k) for i in range(size)])


def local(blocks, block_owner, block_basis, pair_images, pair_cell, lattice, dens_occ, dens_virt):
    owners, images = lax.axis_size("ri"), lax.axis_size("image")
    pairs = pair_cell.shape[1]
    cell_count = lattice.shape[0]
    cap = max(2, (2 * blocks.shape[0] + owners - 1) // owners)

    packed = pack(owners, cap, blocks, block_owner, block_basis, pair_images, pair_cell)
    order = list(range(owners - 2, 1, -1)) + [owners - 1]
    if owners == 8:
        order = [6, 2, 4, 7, 3, 5]
    payload = {0: packed[0]}
    half = len(order) // 2
    payload.update({k: swap(packed[k], "ri", k) for k in order[:half]})
    for k, after in zip(order[half:], order[:half]):
        payload[after], later = lax.optimization_barrier((payload[after], packed[k]))
        payload[k] = swap(later, "ri", k)
    payload[1] = swap(packed[1], "ri", 1)
    density = jnp.concatenate([dens_occ[0].T, dens_virt[0].T], axis=0)
    pieces = density[None]
    k = 1
    while k < images:
        pieces = jnp.concatenate([pieces, swap(pieces, "image", k)], axis=0)
        k = 2 * k
    pieces = [pieces[i] for i in range(images)]

    arrival = [0, 1] + order
    early, late = arrival[: half + 2], arrival[half + 2 :]
    parts = [early[at : at + PART] for at in range(0, len(early), PART)]
    parts += [late[at : at + PART] for at in range(0, len(late), PART)]
    chi = None
    for part in parts:
        out = chi_part(
            cap, pairs, cell_count, [payload[k] for k in part], pieces, chi, part is parts[-1]
        )
        chi = out[0]
    own, sends = out[0], out[1:]
    received = [swap(sends[k - 1], "image", k) for k in range(1, images)]

    points = jnp.arange(KGRID * KGRID, dtype=jnp.int32)
    wrapped = (
        lattice[:, 0:1] * (points // KGRID)[None, :] + lattice[:, 1:2] * (points % KGRID)[None, :]
    ) % KGRID
    angles = 2.0 * math.pi / KGRID * wrapped.astype(F32)
    phases = jnp.concatenate([jnp.cos(angles), jnp.sin(angles)], axis=1)
    result = transform(phases, own, received)
    return result.reshape(2, KGRID * KGRID, 1, own.shape[1], own.shape[2])


def solution(mesh):
    placed = (
        P(("image", "ri"), None, None),
        P(("image", "ri"), None),
        P(("image", "ri"), None),
        P(("image", "ri"), None, None),
        P(("image", "ri"), None),
        P(),
        P("image", None, None),
        P("image", None, None),
    )
    return jax.shard_map(
        local,
        mesh=mesh,
        in_specs=placed,
        out_specs=P(None, None, "ri", "image", None),
        check_vma=False,
    )
```

```python
import functools
import math

import jax
import jax.numpy as jnp
from jax import lax
from jax.experimental import pallas as pl
from jax.experimental.pallas import tpu as pltpu
from jax.sharding import PartitionSpec as P

KGRID = 8
PART = 5
QUAD = 4
LIST_ROWS = 16
BF16 = jnp.bfloat16
F32 = jnp.float32
VMEM_LIMIT = 48 * 1024 * 1024
CHI_FLOPS, CHI_BYTES = 1 << 20, 1 << 10
PACK_LIMIT = 48 * 1024 * 1024


def iota(shape, dim):
    return lax.broadcasted_iota(jnp.int32, shape, dim)


def dot(a, b, contract=(1, 0)):
    return lax.dot_general(
        a, b, (((contract[0],), (contract[1],)), ((), ())), preferred_element_type=F32
    )


def lists_with(k):
    if k < 2:
        return [k]
    return [k, k ^ 1] if k % 2 == 0 else []


def pack_kernel(n, cap, pairs, *refs):
    ints, from_blocks, outs, rest = refs[0], refs[1], refs[2 : 2 + n], refs[2 + n :]
    owner, blocks, table, lists, count, place, sems = rest
    rows, square, width = blocks.shape
    me = lax.axis_index("ri")
    pieces = 4
    part = rows // pieces
    started = [pltpu.make_async_copy(ints.at[pl.ds(0, 8)], owner, sems.at[pieces])]
    for i in range(pieces):
        at = pl.ds(i * part, part)
        started.append(pltpu.make_async_copy(from_blocks.at[at], blocks.at[at], sems.at[i]))
    for copy in started:
        copy.start()
    for k in range(n):
        count[k] = 0
    for k in range(n * cap):
        place[k] = 0
    table[...] = jnp.zeros_like(table)
    lists[...] = jnp.zeros_like(lists)

    distance = ints[0:1, :] ^ me
    as_column = jnp.sum(
        jnp.where(iota((rows, rows), 0) == iota((rows, rows), 1), distance, 0),
        axis=1,
        keepdims=True,
    )
    before = (as_column == distance) & (iota((rows, rows), 0) < iota((rows, rows), 1))
    rank = jnp.sum(before.astype(jnp.int32), axis=0, keepdims=True)
    chosen = iota((n * LIST_ROWS, rows), 0) == distance * LIST_ROWS + rank
    table[0 : ints.shape[0], :] = ints[...].astype(F32)
    table[ints.shape[0] - pairs : ints.shape[0], :] += 1.0
    ordered = dot(chosen.astype(BF16), table[...].astype(BF16), (1, 1))
    lists[:, 0:128] = ordered.astype(BF16)

    started[0].wait()

    @pl.loop(0, rows, unroll=4)
    def _(e):
        k = owner[0, e] ^ me
        r = count[k]
        place[k * cap + r] = e
        count[k] = r + 1

    for copy in started[1:]:
        copy.wait()
    for k in range(n):
        for r in range(cap):
            outs[k][r * square : (r + 1) * square, :] = blocks[place[k * cap + r]]
        for i, of in enumerate(lists_with(k)):
            at = cap * square + i * LIST_ROWS
            outs[k][at : at + LIST_ROWS, :] = lists[of * LIST_ROWS : (of + 1) * LIST_ROWS, :]


def pack(n, cap, blocks, block_owner, block_basis, pair_images, pair_cell):
    rows, square, width = blocks.shape
    pairs = pair_cell.shape[1]
    ints = jnp.concatenate(
        [
            block_owner.T,
            block_basis.T,
            jnp.transpose(pair_images, (1, 2, 0)).reshape(2 * pairs, rows),
            pair_cell.T,
        ],
        axis=0,
    )
    heights = [cap * square + len(lists_with(k)) * LIST_ROWS for k in range(n)]
    return pl.pallas_call(
        functools.partial(pack_kernel, n, cap, pairs),
        out_shape=[jax.ShapeDtypeStruct((height, width), BF16) for height in heights],
        in_specs=[
            pl.BlockSpec(memory_space=pltpu.VMEM),
            pl.BlockSpec(memory_space=pltpu.HBM),
        ],
        out_specs=[pl.BlockSpec(memory_space=pltpu.VMEM)] * n,
        scratch_shapes=[
            pltpu.SMEM((8, rows), jnp.int32),
            pltpu.VMEM(blocks.shape, BF16),
            pltpu.VMEM((128, rows), F32),
            pltpu.VMEM((n * LIST_ROWS, width), BF16),
            pltpu.SMEM((n,), jnp.int32),
            pltpu.SMEM((n * cap,), jnp.int32),
            pltpu.SemaphoreType.DMA((5,)),
        ],
        compiler_params=pltpu.CompilerParams(vmem_limit_bytes=PACK_LIMIT),
        cost_estimate=pl.CostEstimate(flops=0, bytes_accessed=6 << 20, transcendentals=0),
        name="pack_by_owner",
    )(ints, blocks)


def by_halving(images):
    return images == 4


def shares_of(images):
    kept = [(part, [0], F32) for part in range(2)]
    if by_halving(images):
        kept += [(1, [2], F32), (1, [1, 3], BF16)]
        return kept + [(0, [k], BF16) for k in (2, 3, 1)]
    return kept + [(part, [k], BF16) for part in range(2) for k in range(1, images)]


def diagonals(cap, pairs, cell_count, side, lists, table):
    images = lax.axis_size("image")
    z = lax.axis_index("image")
    square = side * side
    quad = min(QUAD, cap)
    lanes = quad * square
    height = 8 * len(lists)
    lane = iota((1, lanes), 1)
    listing = jnp.concatenate(
        [ref[at : at + LIST_ROWS, 0:128].astype(F32)[0:8] for ref, at in lists], axis=0
    )

    def columns(start):
        return jnp.concatenate(
            [listing[:, start + j : start + j + 1] for j in range(pairs)], axis=0
        ).astype(jnp.int32)

    def side_by_side(rows, at):
        out = jnp.where(lane // square == 0, rows[at : at + 1], 0.0)
        for s in range(1, quad):
            out = jnp.where(lane // square == s, rows[at + s : at + s + 1], out)
        return out

    def density_rows(basis_at, image_at, lane_at):
        block = jnp.concatenate([listing[:, basis_at : basis_at + 1]] * pairs, axis=0)
        row = (columns(image_at) ^ z) * (table.shape[0] // images) + block.astype(jnp.int32)
        chosen = iota((height * pairs, table.shape[0]), 1) == row
        found = dot(jnp.where(chosen, 1.0, 0.0).astype(BF16), table[...])
        return jnp.concatenate([found[:, lane_at : lane_at + square]] * quad, axis=1)

    occ = density_rows(1, 3, 0)
    virt = density_rows(2, 3 + pairs, square)
    cell = jnp.broadcast_to(columns(3 + 2 * pairs).astype(F32), (height * pairs, lanes))

    shape = (square, lanes)
    occ_mask = (iota(shape, 1) % side == iota(shape, 0) // side).astype(BF16)
    virt_mask = (iota(shape, 1) % square // side == iota(shape, 0) % side).astype(BF16)
    shape = (lanes, lanes)
    occ_spread = (iota(shape, 0) // side == iota(shape, 1) // side).astype(BF16)
    virt_spread = (
        (iota(shape, 0) // square == iota(shape, 1) // square)
        & (iota(shape, 0) % side == iota(shape, 1) % side)
    ).astype(BF16)

    for p in range(len(lists)):
        for g in range(cap // quad):
            at = [j * height + 8 * p + g * quad for j in range(pairs)]
            occ_in = jnp.concatenate(
                [occ_mask * side_by_side(occ, a).astype(BF16) for a in at], axis=0
            )
            virt_in = jnp.concatenate(
                [virt_mask * side_by_side(virt, a).astype(BF16) for a in at], axis=0
            )
            terms = dot(occ_in, occ_spread) * dot(virt_in, virt_spread)
            here = [side_by_side(cell, a) for a in at]
            out = []
            for c in range(cell_count):
                op = None
                for j in range(pairs):
                    term = terms[j * square : (j + 1) * square]
                    term = jnp.where(here[j] == float(c + 1), term, 0.0)
                    op = term if op is None else op + term
                out.append(
                    jnp.concatenate(
                        [jnp.where(lane // square == s, op, 0.0) for s in range(quad)], axis=0
                    ).astype(BF16)
                )
            yield out


def early_kernel(count, cap, pairs, cell_count, square, first, *refs):
    refs = list(refs)
    images = lax.axis_size("image")
    payloads = [refs.pop(0) for _ in range(count)]
    if first:
        pieces = [refs.pop(0) for _ in range(images)]
        total, table, mixed, stacked = refs
        for i in range(images):
            block_count = pieces[i].shape[1]
            table[i * block_count : (i + 1) * block_count, :] = pieces[i][...].T
        before = None
    else:
        before, table, total, mixed, stacked = refs
    lists = [(p, cap * square) for p in payloads]
    made = diagonals(cap, pairs, cell_count, math.isqrt(square), lists, table)
    add_blocks(cap, square, payloads, made, before, total, mixed, stacked)


def add_blocks(cap, square, payloads, made, before, total, mixed, stacked):
    lanes = min(QUAD, cap) * square
    per = cap * square // lanes
    for i, operators in enumerate(made):
        p, g = divmod(i, per)
        block = payloads[p][g * lanes : (g + 1) * lanes, :]
        stacked[i * lanes : (i + 1) * lanes, :] = block
        turned = block.T
        for c, operator in enumerate(operators):
            mixed[c, :, i * lanes : (i + 1) * lanes] = dot(turned, operator).astype(BF16)
    for c in range(mixed.shape[0]):
        acc = dot(mixed[c], stacked[...])
        total[c] = acc if before is None else acc + before[c]


def operators_kernel(count, cap, pairs, cell_count, square, lists, table, out):
    places = [(lists, i * LIST_ROWS) for i in range(count)]
    made = diagonals(cap, pairs, cell_count, math.isqrt(square), places, table)
    for i, operators in enumerate(made):
        for c in range(cell_count):
            out[i * cell_count + c] = operators[c]


def late_kernel(count, cap, cell_count, square, last, *refs):
    refs = list(refs)
    images = lax.axis_size("image")
    payloads = [refs.pop(0) for _ in range(count)]
    before, operators = refs.pop(0), refs.pop(0)
    outs = [refs.pop(0) for _ in shares_of(images)] if last else []
    total, mixed, stacked = refs
    made = (
        [operators[i * cell_count + c] for c in range(cell_count)]
        for i in range(operators.shape[0] // cell_count)
    )
    add_blocks(cap, square, payloads, made, before, total, mixed, stacked)
    if last:
        z = lax.axis_index("image")
        half = outs[0].shape[1]
        for ref, (part, distances, _) in zip(outs, shares_of(images)):
            for i, k in enumerate(distances):
                at = pl.multiple_of((z ^ k) * (2 * half) + part * half, half)
                taken = total[:, pl.ds(at, half), :].astype(ref.dtype)
                if len(distances) == 1:
                    ref[...] = taken
                else:
                    ref[i * cell_count : (i + 1) * cell_count] = taken


def on_chip(kernel, name, args, out_shape, scratch=()):
    vmem = pl.BlockSpec(memory_space=pltpu.VMEM)
    return pl.pallas_call(
        kernel,
        out_shape=out_shape,
        in_specs=[vmem] * len(args),
        out_specs=[vmem] * len(out_shape),
        scratch_shapes=list(scratch),
        compiler_params=pltpu.CompilerParams(vmem_limit_bytes=VMEM_LIMIT),
        cost_estimate=pl.CostEstimate(
            flops=CHI_FLOPS, bytes_accessed=CHI_BYTES, transcendentals=0
        ),
        name=name,
    )(*args)


def chi_scratch(cell_count, width, depth):
    return [pltpu.VMEM((cell_count, width, depth), BF16), pltpu.VMEM((depth, width), BF16)]


def early_part(cap, pairs, cell_count, square, payloads, given, first):
    count, width = len(payloads), payloads[0].shape[1]
    out_shape = [jax.ShapeDtypeStruct((cell_count, width, width), F32)]
    if first:
        shape = (len(given) * given[0].shape[1], given[0].shape[0])
        out_shape.append(jax.ShapeDtypeStruct(shape, BF16))
    return on_chip(
        functools.partial(early_kernel, count, cap, pairs, cell_count, square, first),
        "chi_of_early_payloads",
        list(payloads) + list(given),
        out_shape,
        chi_scratch(cell_count, width, count * cap * square),
    )


def operators_part(cap, pairs, cell_count, square, lists, table):
    count = lists.shape[0] // LIST_ROWS
    lanes = min(QUAD, cap) * square
    groups = count * cap * square // lanes
    return on_chip(
        functools.partial(operators_kernel, count, cap, pairs, cell_count, square),
        "operators_of_late_payloads",
        [lists, table],
        [jax.ShapeDtypeStruct((groups * cell_count, lanes, lanes), BF16)],
    )[0]


def late_part(cap, cell_count, square, images, payloads, before, operators, last):
    count, width = len(payloads), payloads[0].shape[1]
    full = (cell_count, width, width)
    scratch = chi_scratch(cell_count, width, count * cap * square)
    out_shape = [jax.ShapeDtypeStruct(full, F32)]
    if last:
        half = width // images // 2
        out_shape = [
            jax.ShapeDtypeStruct((len(distances) * cell_count, half, width), dtype)
            for _, distances, dtype in shares_of(images)
        ]
        scratch = [pltpu.VMEM(full, F32)] + scratch
    return on_chip(
        functools.partial(late_kernel, count, cap, cell_count, square, last),
        "chi_of_late_payloads",
        list(payloads) + [before, operators],
        out_shape,
        scratch,
    )


def transform_kernel(cell_count, step, counts, phases, *refs):
    refs = list(refs)
    halves = [[refs.pop(0) for _ in range(n)] for n in counts]
    out, total, shaped, sems = refs
    for i, (own, *received) in enumerate(halves):
        acc = own[...]
        for part in received:
            acc = acc + part[0:cell_count].astype(F32)
        total[:, i * acc.shape[1] : (i + 1) * acc.shape[1], :] = acc
    points, share, width = out.shape
    tile = min(share, 32)

    def copy(i):
        at = pl.ds(i * step, step)
        return pltpu.make_async_copy(shaped.at[at], out.at[at], sems.at[i])

    @pl.loop(0, points // step)
    def _(i):
        for row in range(0, share, tile):
            parts = [total[c, row : row + tile, :] for c in range(cell_count)]
            for j in range(step):
                acc = phases[0, i * step + j] * parts[0]
                for c in range(1, cell_count):
                    acc = acc + phases[c, i * step + j] * parts[c]
                shaped[i * step + j, row : row + tile, :] = acc
        copy(i).start()

    @pl.loop(0, points // step)
    def _(i):
        copy(i).wait()


def transform(phases, halves):
    cell_count, rows, width = halves[0][0].shape
    share = rows * len(halves)
    points = phases.shape[1]
    step = 8
    vmem = pl.BlockSpec(memory_space=pltpu.VMEM)
    args = [x for half in halves for x in half]
    return pl.pallas_call(
        functools.partial(transform_kernel, cell_count, step, [len(half) for half in halves]),
        out_shape=jax.ShapeDtypeStruct((points, share, width), F32),
        in_specs=[pl.BlockSpec(memory_space=pltpu.SMEM)] + [vmem] * len(args),
        out_specs=pl.BlockSpec(memory_space=pltpu.HBM),
        scratch_shapes=[
            pltpu.VMEM((cell_count, share, width), F32),
            pltpu.VMEM((points, share, width), F32),
            pltpu.SemaphoreType.DMA((points // step,)),
        ],
        compiler_params=pltpu.CompilerParams(vmem_limit_bytes=VMEM_LIMIT),
        cost_estimate=pl.CostEstimate(
            flops=2 * points * cell_count * share * width,
            bytes_accessed=points * share * width * 4,
            transcendentals=0,
        ),
        name="to_k_points",
    )(phases, *args)


def swap(array, axis, k):
    size = lax.axis_size(axis)
    return lax.ppermute(array, axis, [(i, i ^ k) for i in range(size)])


def local(blocks, block_owner, block_basis, pair_images, pair_cell, lattice, dens_occ, dens_virt):
    owners, images = lax.axis_size("ri"), lax.axis_size("image")
    pairs = pair_cell.shape[1]
    cell_count = lattice.shape[0]
    cap = max(2, (2 * blocks.shape[0] + owners - 1) // owners)

    packed = pack(owners, cap, blocks, block_owner, block_basis, pair_images, pair_cell)
    square = blocks.shape[1]
    evens = [6, 2, 4] if owners == 8 else list(range(owners - 2, 1, -2))
    odds = [k ^ 1 for k in evens]
    payload = {0: packed[0]}
    payload.update({k: swap(packed[k], "ri", k) for k in evens})
    for k in odds:
        payload[k ^ 1], later = lax.optimization_barrier((payload[k ^ 1], packed[k]))
        payload[k] = swap(later, "ri", k)
    payload[evens[0]], near = lax.optimization_barrier((payload[evens[0]], packed[1]))
    payload[1] = swap(near, "ri", 1)
    lists = [payload[k][cap * square + LIST_ROWS :] for k in evens]
    lists = swap(jnp.concatenate(lists, axis=0), "ri", 1)
    density = jnp.concatenate([dens_occ[0].T, dens_virt[0].T], axis=0)
    pieces = density[None]
    k = 1
    while k < images:
        pieces = jnp.concatenate([pieces, swap(pieces, "image", k)], axis=0)
        k = 2 * k
    pieces = [pieces[i] for i in range(images)]

    given = pieces
    early = [0, 1] + evens
    for at in range(0, len(early), PART):
        chosen = [payload[k] for k in early[at : at + PART]]
        out = early_part(cap, pairs, cell_count, square, chosen, given, at == 0)
        table = out[1] if at == 0 else table
        given = [out[0], table]
    chi = out[0]
    for at in range(0, len(odds), PART):
        chosen = [payload[k] for k in odds[at : at + PART]]
        part = lists[at * LIST_ROWS : (at + len(chosen)) * LIST_ROWS]
        operators = operators_part(cap, pairs, cell_count, square, part, table)
        last = at + PART >= len(odds)
        out = late_part(cap, cell_count, square, images, chosen, chi, operators, last)
        chi = out[0]
    halves, sends = [[own] for own in out[:2]], out[2:]
    plan = shares_of(images)[2:]
    if by_halving(images):
        forward, sends, plan = sends[0], sends[1:], plan[1:]
    received = [swap(x, "image", d[0]) for x, (_, d, _) in zip(sends, plan)]
    for x, (part, _, _) in zip(received, plan):
        halves[part].append(x)
    if by_halving(images):
        forward = (forward + received[0][cell_count:].astype(F32)).astype(BF16)
        halves[1].append(swap(forward, "image", 2))

    points = jnp.arange(KGRID * KGRID, dtype=jnp.int32)
    wrapped = (
        lattice[:, 0:1] * (points // KGRID)[None, :] + lattice[:, 1:2] * (points % KGRID)[None, :]
    ) % KGRID
    angles = 2.0 * math.pi / KGRID * wrapped.astype(F32)
    phases = jnp.concatenate([jnp.cos(angles), jnp.sin(angles)], axis=1)
    result = transform(phases, halves)
    return result.reshape((2, KGRID * KGRID, 1) + result.shape[1:])


def solution(mesh):
    placed = (
        P(("image", "ri"), None, None),
        P(("image", "ri"), None),
        P(("image", "ri"), None),
        P(("image", "ri"), None, None),
        P(("image", "ri"), None),
        P(),
        P("image", None, None),
        P("image", None, None),
    )
    return jax.shard_map(
        local,
        mesh=mesh,
        in_specs=placed,
        out_specs=P(None, None, "ri", "image", None),
        check_vma=False,
    )
```

```python
import functools
import math

import jax
import jax.numpy as jnp
from jax import lax
from jax.experimental import pallas as pl
from jax.experimental.pallas import tpu as pltpu
from jax.sharding import PartitionSpec as P

KGRID = 8
PART = 5
QUAD = 4
LIST_ROWS = 16
BF16 = jnp.bfloat16
F32 = jnp.float32
VMEM_LIMIT = 48 * 1024 * 1024
CHI_FLOPS, CHI_BYTES = 1 << 20, 1 << 10
PACK_LIMIT = 48 * 1024 * 1024


def iota(shape, dim):
    return lax.broadcasted_iota(jnp.int32, shape, dim)


def dot(a, b, contract=(1, 0)):
    return lax.dot_general(
        a, b, (((contract[0],), (contract[1],)), ((), ())), preferred_element_type=F32
    )


def lists_with(k):
    if k < 2:
        return [k]
    return [k, k ^ 1] if k % 2 == 0 else []


def pack_kernel(n, cap, pairs, *refs):
    ints, blocks, outs, rest = refs[0], refs[1], refs[2 : 2 + n], refs[2 + n :]
    owner, table, lists, count, place, sem = rest
    rows, square, width = blocks.shape
    me = lax.axis_index("ri")
    to_scalars = pltpu.make_async_copy(ints.at[pl.ds(0, 8)], owner, sem)
    to_scalars.start()
    for k in range(n):
        count[k] = 0
    for k in range(n * cap):
        place[k] = 0
    table[...] = jnp.zeros_like(table)
    lists[...] = jnp.zeros_like(lists)

    distance = ints[0:1, :] ^ me
    as_column = jnp.sum(
        jnp.where(iota((rows, rows), 0) == iota((rows, rows), 1), distance, 0),
        axis=1,
        keepdims=True,
    )
    before = (as_column == distance) & (iota((rows, rows), 0) < iota((rows, rows), 1))
    rank = jnp.sum(before.astype(jnp.int32), axis=0, keepdims=True)
    chosen = iota((n * LIST_ROWS, rows), 0) == distance * LIST_ROWS + rank
    table[0 : ints.shape[0], :] = ints[...].astype(F32)
    table[ints.shape[0] - pairs : ints.shape[0], :] += 1.0
    ordered = dot(chosen.astype(BF16), table[...].astype(BF16), (1, 1))
    lists[:, 0:128] = ordered.astype(BF16)

    to_scalars.wait()

    @pl.loop(0, rows, unroll=4)
    def _(e):
        k = owner[0, e] ^ me
        r = count[k]
        place[k * cap + r] = e
        count[k] = r + 1

    for k in range(n):
        for r in range(cap):
            outs[k][r * square : (r + 1) * square, :] = blocks[place[k * cap + r]]
        for i, of in enumerate(lists_with(k)):
            at = cap * square + i * LIST_ROWS
            outs[k][at : at + LIST_ROWS, :] = lists[of * LIST_ROWS : (of + 1) * LIST_ROWS, :]


def pack(n, cap, blocks, block_owner, block_basis, pair_images, pair_cell):
    rows, square, width = blocks.shape
    pairs = pair_cell.shape[1]
    ints = jnp.concatenate(
        [
            block_owner.T,
            block_basis.T,
            jnp.transpose(pair_images, (1, 2, 0)).reshape(2 * pairs, rows),
            pair_cell.T,
        ],
        axis=0,
    )
    heights = [cap * square + len(lists_with(k)) * LIST_ROWS for k in range(n)]
    return pl.pallas_call(
        functools.partial(pack_kernel, n, cap, pairs),
        out_shape=[jax.ShapeDtypeStruct((height, width), BF16) for height in heights],
        in_specs=[pl.BlockSpec(memory_space=pltpu.VMEM)] * 2,
        out_specs=[pl.BlockSpec(memory_space=pltpu.VMEM)] * n,
        scratch_shapes=[
            pltpu.SMEM((8, rows), jnp.int32),
            pltpu.VMEM((128, rows), F32),
            pltpu.VMEM((n * LIST_ROWS, width), BF16),
            pltpu.SMEM((n,), jnp.int32),
            pltpu.SMEM((n * cap,), jnp.int32),
            pltpu.SemaphoreType.DMA,
        ],
        compiler_params=pltpu.CompilerParams(vmem_limit_bytes=PACK_LIMIT),
        cost_estimate=pl.CostEstimate(flops=0, bytes_accessed=6 << 20, transcendentals=0),
        name="pack_by_owner",
    )(ints, blocks)


def by_halving(images):
    return images == 4


def shares_of(images):
    kept = [(part, [0], F32) for part in range(2)]
    if by_halving(images):
        kept += [(1, [2], F32), (1, [1, 3], BF16)]
        return kept + [(0, [k], BF16) for k in (2, 3, 1)]
    return kept + [(part, [k], BF16) for part in range(2) for k in range(1, images)]


def diagonals(cap, pairs, cell_count, side, lists, table):
    images = lax.axis_size("image")
    z = lax.axis_index("image")
    square = side * side
    quad = min(QUAD, cap)
    lanes = quad * square
    height = 8 * len(lists)
    lane = iota((1, lanes), 1)
    listing = jnp.concatenate(
        [ref[at : at + LIST_ROWS, 0:128].astype(F32)[0:8] for ref, at in lists], axis=0
    )

    def columns(start):
        return jnp.concatenate(
            [listing[:, start + j : start + j + 1] for j in range(pairs)], axis=0
        ).astype(jnp.int32)

    def side_by_side(rows, at):
        out = jnp.where(lane // square == 0, rows[at : at + 1], 0.0)
        for s in range(1, quad):
            out = jnp.where(lane // square == s, rows[at + s : at + s + 1], out)
        return out

    def density_rows(basis_at, image_at, lane_at):
        block = jnp.concatenate([listing[:, basis_at : basis_at + 1]] * pairs, axis=0)
        row = (columns(image_at) ^ z) * (table.shape[0] // images) + block.astype(jnp.int32)
        chosen = iota((height * pairs, table.shape[0]), 1) == row
        found = dot(jnp.where(chosen, 1.0, 0.0).astype(BF16), table[...])
        return jnp.concatenate([found[:, lane_at : lane_at + square]] * quad, axis=1)

    occ = density_rows(1, 3, 0)
    virt = density_rows(2, 3 + pairs, square)
    cell = jnp.broadcast_to(columns(3 + 2 * pairs).astype(F32), (height * pairs, lanes))

    shape = (square, lanes)
    occ_mask = (iota(shape, 1) % side == iota(shape, 0) // side).astype(BF16)
    virt_mask = (iota(shape, 1) % square // side == iota(shape, 0) % side).astype(BF16)
    shape = (lanes, lanes)
    occ_spread = (iota(shape, 0) // side == iota(shape, 1) // side).astype(BF16)
    virt_spread = (
        (iota(shape, 0) // square == iota(shape, 1) // square)
        & (iota(shape, 0) % side == iota(shape, 1) % side)
    ).astype(BF16)

    for p in range(len(lists)):
        for g in range(cap // quad):
            at = [j * height + 8 * p + g * quad for j in range(pairs)]
            occ_in = jnp.concatenate(
                [occ_mask * side_by_side(occ, a).astype(BF16) for a in at], axis=0
            )
            virt_in = jnp.concatenate(
                [virt_mask * side_by_side(virt, a).astype(BF16) for a in at], axis=0
            )
            terms = dot(occ_in, occ_spread) * dot(virt_in, virt_spread)
            here = [side_by_side(cell, a) for a in at]
            out = []
            for c in range(cell_count):
                op = None
                for j in range(pairs):
                    term = terms[j * square : (j + 1) * square]
                    term = jnp.where(here[j] == float(c + 1), term, 0.0)
                    op = term if op is None else op + term
                out.append(
                    jnp.concatenate(
                        [jnp.where(lane // square == s, op, 0.0) for s in range(quad)], axis=0
                    ).astype(BF16)
                )
            yield out


def early_kernel(count, cap, pairs, cell_count, square, first, *refs):
    refs = list(refs)
    images = lax.axis_size("image")
    payloads = [refs.pop(0) for _ in range(count)]
    if first:
        pieces = [refs.pop(0) for _ in range(images)]
        total, table, mixed, stacked = refs
        for i in range(images):
            block_count = pieces[i].shape[1]
            table[i * block_count : (i + 1) * block_count, :] = pieces[i][...].T
        before = None
    else:
        before, table, total, mixed, stacked = refs
    lists = [(p, cap * square) for p in payloads]
    made = diagonals(cap, pairs, cell_count, math.isqrt(square), lists, table)
    add_blocks(cap, square, payloads, made, before, total, mixed, stacked)


def add_blocks(cap, square, payloads, made, before, total, mixed, stacked):
    lanes = min(QUAD, cap) * square
    per = cap * square // lanes
    for i, operators in enumerate(made):
        p, g = divmod(i, per)
        block = payloads[p][g * lanes : (g + 1) * lanes, :]
        stacked[i * lanes : (i + 1) * lanes, :] = block
        turned = block.T
        for c, operator in enumerate(operators):
            mixed[c, :, i * lanes : (i + 1) * lanes] = dot(turned, operator).astype(BF16)
    for c in range(mixed.shape[0]):
        acc = dot(mixed[c], stacked[...])
        total[c] = acc if before is None else acc + before[c]


def operators_kernel(count, cap, pairs, cell_count, square, lists, table, out):
    places = [(lists, i * LIST_ROWS) for i in range(count)]
    made = diagonals(cap, pairs, cell_count, math.isqrt(square), places, table)
    for i, operators in enumerate(made):
        for c in range(cell_count):
            out[i * cell_count + c] = operators[c]


def late_kernel(count, cap, cell_count, square, last, *refs):
    refs = list(refs)
    images = lax.axis_size("image")
    payloads = [refs.pop(0) for _ in range(count)]
    before, operators = refs.pop(0), refs.pop(0)
    outs = [refs.pop(0) for _ in shares_of(images)] if last else []
    total, mixed, stacked = refs
    made = (
        [operators[i * cell_count + c] for c in range(cell_count)]
        for i in range(operators.shape[0] // cell_count)
    )
    add_blocks(cap, square, payloads, made, before, total, mixed, stacked)
    if last:
        z = lax.axis_index("image")
        half = outs[0].shape[1]
        for ref, (part, distances, _) in zip(outs, shares_of(images)):
            for i, k in enumerate(distances):
                at = pl.multiple_of((z ^ k) * (2 * half) + part * half, half)
                taken = total[:, pl.ds(at, half), :].astype(ref.dtype)
                if len(distances) == 1:
                    ref[...] = taken
                else:
                    ref[i * cell_count : (i + 1) * cell_count] = taken


def on_chip(kernel, name, args, out_shape, scratch=()):
    vmem = pl.BlockSpec(memory_space=pltpu.VMEM)
    return pl.pallas_call(
        kernel,
        out_shape=out_shape,
        in_specs=[vmem] * len(args),
        out_specs=[vmem] * len(out_shape),
        scratch_shapes=list(scratch),
        compiler_params=pltpu.CompilerParams(vmem_limit_bytes=VMEM_LIMIT),
        cost_estimate=pl.CostEstimate(
            flops=CHI_FLOPS, bytes_accessed=CHI_BYTES, transcendentals=0
        ),
        name=name,
    )(*args)


def chi_scratch(cell_count, width, depth):
    return [pltpu.VMEM((cell_count, width, depth), BF16), pltpu.VMEM((depth, width), BF16)]


def early_part(cap, pairs, cell_count, square, payloads, given, first):
    count, width = len(payloads), payloads[0].shape[1]
    out_shape = [jax.ShapeDtypeStruct((cell_count, width, width), F32)]
    if first:
        shape = (len(given) * given[0].shape[1], given[0].shape[0])
        out_shape.append(jax.ShapeDtypeStruct(shape, BF16))
    return on_chip(
        functools.partial(early_kernel, count, cap, pairs, cell_count, square, first),
        "chi_of_early_payloads",
        list(payloads) + list(given),
        out_shape,
        chi_scratch(cell_count, width, count * cap * square),
    )


def operators_part(cap, pairs, cell_count, square, lists, table):
    count = lists.shape[0] // LIST_ROWS
    lanes = min(QUAD, cap) * square
    groups = count * cap * square // lanes
    return on_chip(
        functools.partial(operators_kernel, count, cap, pairs, cell_count, square),
        "operators_of_late_payloads",
        [lists, table],
        [jax.ShapeDtypeStruct((groups * cell_count, lanes, lanes), BF16)],
    )[0]


def late_part(cap, cell_count, square, images, payloads, before, operators, last):
    count, width = len(payloads), payloads[0].shape[1]
    full = (cell_count, width, width)
    scratch = chi_scratch(cell_count, width, count * cap * square)
    out_shape = [jax.ShapeDtypeStruct(full, F32)]
    if last:
        half = width // images // 2
        out_shape = [
            jax.ShapeDtypeStruct((len(distances) * cell_count, half, width), dtype)
            for _, distances, dtype in shares_of(images)
        ]
        scratch = [pltpu.VMEM(full, F32)] + scratch
    return on_chip(
        functools.partial(late_kernel, count, cap, cell_count, square, last),
        "chi_of_late_payloads",
        list(payloads) + [before, operators],
        out_shape,
        scratch,
    )


def transform_kernel(cell_count, step, row_at, phases, own, *rest):
    *received, out, total, shaped, sems = rest
    acc = own[...]
    for part in received:
        acc = acc + part[0:cell_count].astype(F32)
    total[...] = acc
    points, rows, width = shaped.shape

    def copy(i):
        at = pl.ds(i * step, step)
        return pltpu.make_async_copy(
            shaped.at[at], out.at[at, pl.ds(row_at, rows)], sems.at[i]
        )

    @pl.loop(0, points // step)
    def _(i):
        parts = [total[c] for c in range(cell_count)]
        for j in range(step):
            acc = phases[0, i * step + j] * parts[0]
            for c in range(1, cell_count):
                acc = acc + phases[c, i * step + j] * parts[c]
            shaped[i * step + j] = acc
        copy(i).start()

    @pl.loop(0, points // step)
    def _(i):
        copy(i).wait()


def transform(phases, own, received, row_at, share, so_far):
    cell_count, rows, width = own.shape
    points = phases.shape[1]
    step = 16
    vmem = pl.BlockSpec(memory_space=pltpu.VMEM)
    hbm = pl.BlockSpec(memory_space=pltpu.HBM)
    args = [phases, own, *received]
    specs = [pl.BlockSpec(memory_space=pltpu.SMEM)] + [vmem] * (1 + len(received))
    aliases = {}
    kernel = functools.partial(transform_kernel, cell_count, step, row_at)
    if so_far is not None:
        aliases = {len(args): 0}
        inner = kernel
        at = len(args)

        def kernel(*refs):
            inner(*refs[:at], *refs[at + 1 :])

        args.append(so_far)
        specs.append(hbm)
    return pl.pallas_call(
        kernel,
        out_shape=jax.ShapeDtypeStruct((points, share, width), F32),
        in_specs=specs,
        out_specs=hbm,
        input_output_aliases=aliases,
        scratch_shapes=[
            pltpu.VMEM((cell_count, rows, width), F32),
            pltpu.VMEM((points, rows, width), F32),
            pltpu.SemaphoreType.DMA((points // step,)),
        ],
        compiler_params=pltpu.CompilerParams(vmem_limit_bytes=VMEM_LIMIT),
        cost_estimate=pl.CostEstimate(
            flops=2 * points * cell_count * rows * width,
            bytes_accessed=points * rows * width * 4,
            transcendentals=0,
        ),
        name="to_k_points",
    )(*args)


def swap(array, axis, k):
    size = lax.axis_size(axis)
    return lax.ppermute(array, axis, [(i, i ^ k) for i in range(size)])


def local(blocks, block_owner, block_basis, pair_images, pair_cell, lattice, dens_occ, dens_virt):
    owners, images = lax.axis_size("ri"), lax.axis_size("image")
    pairs = pair_cell.shape[1]
    cell_count = lattice.shape[0]
    cap = max(2, (2 * blocks.shape[0] + owners - 1) // owners)

    packed = pack(owners, cap, blocks, block_owner, block_basis, pair_images, pair_cell)
    square = blocks.shape[1]
    evens = [6, 2, 4] if owners == 8 else list(range(owners - 2, 1, -2))
    odds = [k ^ 1 for k in evens]
    payload = {0: packed[0]}
    payload.update({k: swap(packed[k], "ri", k) for k in evens})
    for k in odds:
        payload[k ^ 1], later = lax.optimization_barrier((payload[k ^ 1], packed[k]))
        payload[k] = swap(later, "ri", k)
    payload[1], dens_occ, dens_virt = lax.optimization_barrier(
        (swap(packed[1], "ri", 1), dens_occ, dens_virt)
    )
    lists = [payload[k][cap * square + LIST_ROWS :] for k in evens]
    lists = swap(jnp.concatenate(lists, axis=0), "ri", 1)
    density = jnp.concatenate([dens_occ[0].T, dens_virt[0].T], axis=0)
    pieces = density[None]
    k = 1
    while k < images:
        pieces = jnp.concatenate([pieces, swap(pieces, "image", k)], axis=0)
        k = 2 * k
    pieces = [pieces[i] for i in range(images)]

    given = pieces
    early = [0, 1] + evens
    for at in range(0, len(early), PART):
        chosen = [payload[k] for k in early[at : at + PART]]
        out = early_part(cap, pairs, cell_count, square, chosen, given, at == 0)
        table = out[1] if at == 0 else table
        given = [out[0], table]
    chi = out[0]
    for at in range(0, len(odds), PART):
        chosen = [payload[k] for k in odds[at : at + PART]]
        part = lists[at * LIST_ROWS : (at + len(chosen)) * LIST_ROWS]
        operators = operators_part(cap, pairs, cell_count, square, part, table)
        last = at + PART >= len(odds)
        out = late_part(cap, cell_count, square, images, chosen, chi, operators, last)
        chi = out[0]
    halves, sends = [[own] for own in out[:2]], out[2:]
    plan = shares_of(images)[2:]
    if by_halving(images):
        forward, sends, plan = sends[0], sends[1:], plan[1:]
    received = [swap(x, "image", d[0]) for x, (_, d, _) in zip(sends, plan)]
    for x, (part, _, _) in zip(received, plan):
        halves[part].append(x)
    if by_halving(images):
        forward = (forward + received[0][cell_count:].astype(F32)).astype(BF16)
        halves[1].append(swap(forward, "image", 2))

    points = jnp.arange(KGRID * KGRID, dtype=jnp.int32)
    wrapped = (
        lattice[:, 0:1] * (points // KGRID)[None, :] + lattice[:, 1:2] * (points % KGRID)[None, :]
    ) % KGRID
    angles = 2.0 * math.pi / KGRID * wrapped.astype(F32)
    phases = jnp.concatenate([jnp.cos(angles), jnp.sin(angles)], axis=1)
    result = None
    share = 2 * halves[0][0].shape[1]
    for part, (own, *received) in enumerate(halves):
        result = transform(phases, own, received, part * share // 2, share, result)
    return result.reshape((2, KGRID * KGRID, 1) + result.shape[1:])


def solution(mesh):
    placed = (
        P(("image", "ri"), None, None),
        P(("image", "ri"), None),
        P(("image", "ri"), None),
        P(("image", "ri"), None, None),
        P(("image", "ri"), None),
        P(),
        P("image", None, None),
        P("image", None, None),
    )
    return jax.shard_map(
        local,
        mesh=mesh,
        in_specs=placed,
        out_specs=P(None, None, "ri", "image", None),
        check_vma=False,
    )
```

```python
import functools
import math

import jax
import jax.numpy as jnp
from jax import lax
from jax.experimental import pallas as pl
from jax.experimental.pallas import tpu as pltpu
from jax.sharding import PartitionSpec as P

KGRID = 8
PART = 5
DIRECT_ROWS = 32
QUAD = 4
LIST_ROWS = 16
BF16 = jnp.bfloat16
F32 = jnp.float32
VMEM_LIMIT = 48 * 1024 * 1024
CHI_FLOPS, CHI_BYTES = 1 << 20, 1 << 10
PACK_LIMIT = 48 * 1024 * 1024


def iota(shape, dim):
    return lax.broadcasted_iota(jnp.int32, shape, dim)


def dot(a, b, contract=(1, 0)):
    return lax.dot_general(
        a, b, (((contract[0],), (contract[1],)), ((), ())), preferred_element_type=F32
    )


def list_height(k):
    return LIST_ROWS if k < 2 or k % 2 == 0 else 0


def pack_kernel(n, cap, pairs, *refs):
    ints, blocks, outs, rest = refs[0], refs[1], refs[2 : 2 + n], refs[2 + n :]
    owner, table, lists, count, place, sem = rest
    rows, square, width = blocks.shape
    me = lax.axis_index("ri")
    to_scalars = pltpu.make_async_copy(ints.at[pl.ds(0, 8)], owner, sem)
    to_scalars.start()
    for k in range(n):
        count[k] = 0
    for k in range(n * cap):
        place[k] = 0
    table[...] = jnp.zeros_like(table)
    lists[...] = jnp.zeros_like(lists)

    distance = ints[0:1, :] ^ me
    as_column = jnp.sum(
        jnp.where(iota((rows, rows), 0) == iota((rows, rows), 1), distance, 0),
        axis=1,
        keepdims=True,
    )
    before = (as_column == distance) & (iota((rows, rows), 0) < iota((rows, rows), 1))
    rank = jnp.sum(before.astype(jnp.int32), axis=0, keepdims=True)
    odd = jnp.where(distance < 2, 0, distance % 2)
    place_of = (distance - odd) * LIST_ROWS + odd * 8 + rank
    chosen = iota((n * LIST_ROWS, rows), 0) == place_of
    table[0 : ints.shape[0], :] = ints[...].astype(F32)
    table[ints.shape[0] - pairs : ints.shape[0], :] += 1.0
    ordered = dot(chosen.astype(BF16), table[...].astype(BF16), (1, 1))
    lists[:, 0:128] = ordered.astype(BF16)

    to_scalars.wait()

    @pl.loop(0, rows, unroll=4)
    def _(e):
        k = owner[0, e] ^ me
        r = count[k]
        place[k * cap + r] = e
        count[k] = r + 1

    for k in range(n):
        for r in range(cap):
            outs[k][r * square : (r + 1) * square, :] = blocks[place[k * cap + r]]
        if list_height(k) > 0:
            outs[k][cap * square :, :] = lists[k * LIST_ROWS : (k + 1) * LIST_ROWS, :]


def pack(n, cap, blocks, block_owner, block_basis, pair_images, pair_cell):
    rows, square, width = blocks.shape
    pairs = pair_cell.shape[1]
    ints = jnp.concatenate(
        [
            block_owner.T,
            block_basis.T,
            jnp.transpose(pair_images, (1, 2, 0)).reshape(2 * pairs, rows),
            pair_cell.T,
        ],
        axis=0,
    )
    heights = [cap * square + list_height(k) for k in range(n)]
    return pl.pallas_call(
        functools.partial(pack_kernel, n, cap, pairs),
        out_shape=[jax.ShapeDtypeStruct((height, width), BF16) for height in heights],
        in_specs=[pl.BlockSpec(memory_space=pltpu.VMEM)] * 2,
        out_specs=[pl.BlockSpec(memory_space=pltpu.VMEM)] * n,
        scratch_shapes=[
            pltpu.SMEM((8, rows), jnp.int32),
            pltpu.VMEM((128, rows), F32),
            pltpu.VMEM((n * LIST_ROWS, width), BF16),
            pltpu.SMEM((n,), jnp.int32),
            pltpu.SMEM((n * cap,), jnp.int32),
            pltpu.SemaphoreType.DMA,
        ],
        compiler_params=pltpu.CompilerParams(vmem_limit_bytes=PACK_LIMIT),
        cost_estimate=pl.CostEstimate(flops=0, bytes_accessed=6 << 20, transcendentals=0),
        name="pack_by_owner",
    )(ints, blocks)


def by_halving(images):
    return images == 4


def row_parts(images, share):
    if by_halving(images):
        return [(0, DIRECT_ROWS), (DIRECT_ROWS, share - DIRECT_ROWS)]
    return [(0, share)]


def shares_of(images):
    if not by_halving(images):
        return [(0, [0], F32)] + [(0, [k], BF16) for k in range(1, images)]
    kept = [(0, [0], F32), (1, [0], F32), (1, [2], F32), (1, [1, 3], BF16)]
    return kept + [(0, [k], BF16) for k in (2, 3, 1)]


def diagonals(cap, pairs, cell_count, side, lists, table):
    images = lax.axis_size("image")
    z = lax.axis_index("image")
    square = side * side
    quad = min(QUAD, cap)
    lanes = quad * square
    height = 8 * len(lists)
    lane = iota((1, lanes), 1)
    listing = jnp.concatenate(
        [ref[at : at + LIST_ROWS, 0:128].astype(F32)[i : i + 8] for ref, at, i in lists], axis=0
    )

    def columns(start):
        return jnp.concatenate(
            [listing[:, start + j : start + j + 1] for j in range(pairs)], axis=0
        ).astype(jnp.int32)

    def side_by_side(rows, at):
        out = jnp.where(lane // square == 0, rows[at : at + 1], 0.0)
        for s in range(1, quad):
            out = jnp.where(lane // square == s, rows[at + s : at + s + 1], out)
        return out

    def density_rows(basis_at, image_at, lane_at):
        block = jnp.concatenate([listing[:, basis_at : basis_at + 1]] * pairs, axis=0)
        row = (columns(image_at) ^ z) * (table.shape[0] // images) + block.astype(jnp.int32)
        chosen = iota((height * pairs, table.shape[0]), 1) == row
        found = dot(jnp.where(chosen, 1.0, 0.0).astype(BF16), table[...])
        return jnp.concatenate([found[:, lane_at : lane_at + square]] * quad, axis=1)

    occ = density_rows(1, 3, 0)
    virt = density_rows(2, 3 + pairs, square)
    cell = jnp.broadcast_to(columns(3 + 2 * pairs).astype(F32), (height * pairs, lanes))

    shape = (square, lanes)
    occ_mask = (iota(shape, 1) % side == iota(shape, 0) // side).astype(BF16)
    virt_mask = (iota(shape, 1) % square // side == iota(shape, 0) % side).astype(BF16)
    shape = (lanes, lanes)
    occ_spread = (iota(shape, 0) // side == iota(shape, 1) // side).astype(BF16)
    virt_spread = (
        (iota(shape, 0) // square == iota(shape, 1) // square)
        & (iota(shape, 0) % side == iota(shape, 1) % side)
    ).astype(BF16)

    for p in range(len(lists)):
        for g in range(cap // quad):
            at = [j * height + 8 * p + g * quad for j in range(pairs)]
            occ_in = jnp.concatenate(
                [occ_mask * side_by_side(occ, a).astype(BF16) for a in at], axis=0
            )
            virt_in = jnp.concatenate(
                [virt_mask * side_by_side(virt, a).astype(BF16) for a in at], axis=0
            )
            terms = dot(occ_in, occ_spread) * dot(virt_in, virt_spread)
            here = [side_by_side(cell, a) for a in at]
            out = []
            for c in range(cell_count):
                op = None
                for j in range(pairs):
                    term = terms[j * square : (j + 1) * square]
                    term = jnp.where(here[j] == float(c + 1), term, 0.0)
                    op = term if op is None else op + term
                out.append(
                    jnp.concatenate(
                        [jnp.where(lane // square == s, op, 0.0) for s in range(quad)], axis=0
                    ).astype(BF16)
                )
            yield out


def early_kernel(count, cap, pairs, cell_count, square, first, *refs):
    refs = list(refs)
    images = lax.axis_size("image")
    payloads = [refs.pop(0) for _ in range(count)]
    if first:
        pieces = [refs.pop(0) for _ in range(images)]
        total, table, mixed, stacked = refs
        for i in range(images):
            block_count = pieces[i].shape[1]
            table[i * block_count : (i + 1) * block_count, :] = pieces[i][...].T
        before = None
    else:
        before, table, total, mixed, stacked = refs
    lists = [(p, cap * square, 0) for p in payloads]
    made = diagonals(cap, pairs, cell_count, math.isqrt(square), lists, table)
    add_blocks(cap, square, payloads, made, before, total, mixed, stacked)


def add_blocks(cap, square, payloads, made, before, total, mixed, stacked):
    lanes = min(QUAD, cap) * square
    per = cap * square // lanes
    for i, operators in enumerate(made):
        p, g = divmod(i, per)
        block = payloads[p][g * lanes : (g + 1) * lanes, :]
        stacked[i * lanes : (i + 1) * lanes, :] = block
        turned = block.T
        for c, operator in enumerate(operators):
            mixed[c, :, i * lanes : (i + 1) * lanes] = dot(turned, operator).astype(BF16)
    for c in range(mixed.shape[0]):
        acc = dot(mixed[c], stacked[...])
        total[c] = acc if before is None else acc + before[c]


def operators_kernel(count, cap, pairs, cell_count, square, lists, table, out):
    places = [(lists, i * LIST_ROWS, 8) for i in range(count)]
    made = diagonals(cap, pairs, cell_count, math.isqrt(square), places, table)
    for i, operators in enumerate(made):
        for c in range(cell_count):
            out[i * cell_count + c] = operators[c]


def late_kernel(count, cap, cell_count, square, last, *refs):
    refs = list(refs)
    images = lax.axis_size("image")
    payloads = [refs.pop(0) for _ in range(count)]
    before, operators = refs.pop(0), refs.pop(0)
    outs = [refs.pop(0) for _ in shares_of(images)] if last else []
    total, mixed, stacked = refs
    made = (
        [operators[i * cell_count + c] for c in range(cell_count)]
        for i in range(operators.shape[0] // cell_count)
    )
    add_blocks(cap, square, payloads, made, before, total, mixed, stacked)
    if last:
        z = lax.axis_index("image")
        share = total.shape[1] // images
        parts = row_parts(images, share)
        for ref, (part, distances, _) in zip(outs, shares_of(images)):
            start, rows = parts[part]
            for i, k in enumerate(distances):
                at = pl.multiple_of((z ^ k) * share + start, 16)
                taken = total[:, pl.ds(at, rows), :].astype(ref.dtype)
                if len(distances) == 1:
                    ref[...] = taken
                else:
                    ref[i * cell_count : (i + 1) * cell_count] = taken


def on_chip(kernel, name, args, out_shape, scratch=()):
    vmem = pl.BlockSpec(memory_space=pltpu.VMEM)
    return pl.pallas_call(
        kernel,
        out_shape=out_shape,
        in_specs=[vmem] * len(args),
        out_specs=[vmem] * len(out_shape),
        scratch_shapes=list(scratch),
        compiler_params=pltpu.CompilerParams(vmem_limit_bytes=VMEM_LIMIT),
        cost_estimate=pl.CostEstimate(
            flops=CHI_FLOPS, bytes_accessed=CHI_BYTES, transcendentals=0
        ),
        name=name,
    )(*args)


def chi_scratch(cell_count, width, depth):
    return [pltpu.VMEM((cell_count, width, depth), BF16), pltpu.VMEM((depth, width), BF16)]


def early_part(cap, pairs, cell_count, square, payloads, given, first):
    count, width = len(payloads), payloads[0].shape[1]
    out_shape = [jax.ShapeDtypeStruct((cell_count, width, width), F32)]
    if first:
        shape = (len(given) * given[0].shape[1], given[0].shape[0])
        out_shape.append(jax.ShapeDtypeStruct(shape, BF16))
    return on_chip(
        functools.partial(early_kernel, count, cap, pairs, cell_count, square, first),
        "chi_of_early_payloads",
        list(payloads) + list(given),
        out_shape,
        chi_scratch(cell_count, width, count * cap * square),
    )


def operators_part(cap, pairs, cell_count, square, lists, table):
    count = lists.shape[0] // LIST_ROWS
    lanes = min(QUAD, cap) * square
    groups = count * cap * square // lanes
    return on_chip(
        functools.partial(operators_kernel, count, cap, pairs, cell_count, square),
        "operators_of_late_payloads",
        [lists, table],
        [jax.ShapeDtypeStruct((groups * cell_count, lanes, lanes), BF16)],
    )[0]


def late_part(cap, cell_count, square, images, payloads, before, operators, last):
    count, width = len(payloads), payloads[0].shape[1]
    full = (cell_count, width, width)
    scratch = chi_scratch(cell_count, width, count * cap * square)
    out_shape = [jax.ShapeDtypeStruct(full, F32)]
    if last:
        parts = row_parts(images, width // images)
        out_shape = [
            jax.ShapeDtypeStruct((len(distances) * cell_count, parts[part][1], width), dtype)
            for part, distances, dtype in shares_of(images)
        ]
        scratch = [pltpu.VMEM(full, F32)] + scratch
    return on_chip(
        functools.partial(late_kernel, count, cap, cell_count, square, last),
        "chi_of_late_payloads",
        list(payloads) + [before, operators],
        out_shape,
        scratch,
    )


def transform_kernel(cell_count, step, row_at, phases, own, *rest):
    *received, out, total, shaped, sems = rest
    acc = own[...]
    for part in received:
        acc = acc + part[0:cell_count].astype(F32)
    total[...] = acc
    points, rows, width = shaped.shape

    def copy(i):
        at = pl.ds(i * step, step)
        return pltpu.make_async_copy(
            shaped.at[at], out.at[at, pl.ds(row_at, rows)], sems.at[i]
        )

    @pl.loop(0, points // step)
    def _(i):
        parts = [total[c] for c in range(cell_count)]
        for j in range(step):
            acc = phases[0, i * step + j] * parts[0]
            for c in range(1, cell_count):
                acc = acc + phases[c, i * step + j] * parts[c]
            shaped[i * step + j] = acc
        copy(i).start()

    @pl.loop(0, points // step)
    def _(i):
        copy(i).wait()


def transform(phases, own, received, row_at, share, so_far):
    cell_count, rows, width = own.shape
    points = phases.shape[1]
    step = 16
    vmem = pl.BlockSpec(memory_space=pltpu.VMEM)
    hbm = pl.BlockSpec(memory_space=pltpu.HBM)
    args = [phases, own, *received]
    specs = [pl.BlockSpec(memory_space=pltpu.SMEM)] + [vmem] * (1 + len(received))
    aliases = {}
    kernel = functools.partial(transform_kernel, cell_count, step, row_at)
    if so_far is not None:
        aliases = {len(args): 0}
        inner = kernel
        at = len(args)

        def kernel(*refs):
            inner(*refs[:at], *refs[at + 1 :])

        args.append(so_far)
        specs.append(hbm)
    return pl.pallas_call(
        kernel,
        out_shape=jax.ShapeDtypeStruct((points, share, width), F32),
        in_specs=specs,
        out_specs=hbm,
        input_output_aliases=aliases,
        scratch_shapes=[
            pltpu.VMEM((cell_count, rows, width), F32),
            pltpu.VMEM((points, rows, width), F32),
            pltpu.SemaphoreType.DMA((points // step,)),
        ],
        compiler_params=pltpu.CompilerParams(vmem_limit_bytes=VMEM_LIMIT),
        cost_estimate=pl.CostEstimate(
            flops=2 * points * cell_count * rows * width,
            bytes_accessed=points * rows * width * 4,
            transcendentals=0,
        ),
        name="to_k_points",
    )(*args)


def swap(array, axis, k):
    size = lax.axis_size(axis)
    return lax.ppermute(array, axis, [(i, i ^ k) for i in range(size)])


def local(blocks, block_owner, block_basis, pair_images, pair_cell, lattice, dens_occ, dens_virt):
    owners, images = lax.axis_size("ri"), lax.axis_size("image")
    pairs = pair_cell.shape[1]
    cell_count = lattice.shape[0]
    cap = max(2, (2 * blocks.shape[0] + owners - 1) // owners)

    packed = pack(owners, cap, blocks, block_owner, block_basis, pair_images, pair_cell)
    square = blocks.shape[1]
    evens = [6, 2, 4] if owners == 8 else list(range(owners - 2, 1, -2))
    odds = [k ^ 1 for k in evens]
    payload = {0: packed[0]}
    payload.update({k: swap(packed[k], "ri", k) for k in evens})
    for k in odds:
        payload[k ^ 1], later = lax.optimization_barrier((payload[k ^ 1], packed[k]))
        payload[k] = swap(later, "ri", k)
    payload[1], dens_occ, dens_virt = lax.optimization_barrier(
        (swap(packed[1], "ri", 1), dens_occ, dens_virt)
    )
    lists = [payload[k][cap * square :] for k in evens]
    lists = swap(jnp.concatenate(lists, axis=0), "ri", 1)
    density = jnp.concatenate([dens_occ[0].T, dens_virt[0].T], axis=0)
    pieces = density[None]
    k = 1
    while k < images:
        pieces = jnp.concatenate([pieces, swap(pieces, "image", k)], axis=0)
        k = 2 * k
    pieces = [pieces[i] for i in range(images)]

    given = pieces
    early = [0, 1] + evens
    for at in range(0, len(early), PART):
        chosen = [payload[k] for k in early[at : at + PART]]
        out = early_part(cap, pairs, cell_count, square, chosen, given, at == 0)
        table = out[1] if at == 0 else table
        given = [out[0], table]
    chi = out[0]
    for at in range(0, len(odds), PART):
        chosen = [payload[k] for k in odds[at : at + PART]]
        part = lists[at * LIST_ROWS : (at + len(chosen)) * LIST_ROWS]
        operators = operators_part(cap, pairs, cell_count, square, part, table)
        last = at + PART >= len(odds)
        out = late_part(cap, cell_count, square, images, chosen, chi, operators, last)
        chi = out[0]
    plan = shares_of(images)
    parts = [[x] for x, (_, distances, _) in zip(out, plan) if distances == [0]]
    given = dict(zip([(part, distances[0]) for part, distances, _ in plan], out))
    for part, distances, dtype in plan:
        if dtype == BF16:
            k = distances[0]
            parts[part].append(swap(given[part, k], "image", k))
    if by_halving(images):
        forward = parts[1][1][cell_count:].astype(F32) + given[1, 2]
        parts[1].append(swap(forward.astype(BF16), "image", 2))

    points = jnp.arange(KGRID * KGRID, dtype=jnp.int32)
    wrapped = (
        lattice[:, 0:1] * (points // KGRID)[None, :] + lattice[:, 1:2] * (points % KGRID)[None, :]
    ) % KGRID
    angles = 2.0 * math.pi / KGRID * wrapped.astype(F32)
    phases = jnp.concatenate([jnp.cos(angles), jnp.sin(angles)], axis=1)
    result = None
    share = blocks.shape[2] // images
    places = list(zip(row_parts(images, share), parts))
    for (row_at, _), (own, *received) in places:
        result = transform(phases, own, received, row_at, share, result)
    return result.reshape((2, KGRID * KGRID, 1) + result.shape[1:])


def solution(mesh):
    placed = (
        P(("image", "ri"), None, None),
        P(("image", "ri"), None),
        P(("image", "ri"), None),
        P(("image", "ri"), None, None),
        P(("image", "ri"), None),
        P(),
        P("image", None, None),
        P("image", None, None),
    )
    return jax.shard_map(
        local,
        mesh=mesh,
        in_specs=placed,
        out_specs=P(None, None, "ri", "image", None),
        check_vma=False,
    )
```

```python
import functools
import math

import jax
import jax.numpy as jnp
from jax import lax
from jax.experimental import pallas as pl
from jax.experimental.pallas import tpu as pltpu
from jax.sharding import PartitionSpec as P

KGRID = 8
PART = 5
DIRECT_ROWS = 32
QUAD = 4
LIST_ROWS = 16
BF16 = jnp.bfloat16
F32 = jnp.float32
VMEM_LIMIT = 48 * 1024 * 1024
CHI_FLOPS, CHI_BYTES = 1 << 20, 1 << 10
PACK_LIMIT = 48 * 1024 * 1024


def iota(shape, dim):
    return lax.broadcasted_iota(jnp.int32, shape, dim)


def dot(a, b, contract=(1, 0)):
    return lax.dot_general(
        a, b, (((contract[0],), (contract[1],)), ((), ())), preferred_element_type=F32
    )


def list_height(k):
    return LIST_ROWS if k < 2 or k % 2 == 0 else 0


def pack_kernel(n, cap, pairs, *refs):
    ints, blocks, outs, rest = refs[0], refs[1], refs[2 : 2 + n], refs[2 + n :]
    owner, table, lists, count, place, sem = rest
    rows, square, width = blocks.shape
    me = lax.axis_index("ri")
    to_scalars = pltpu.make_async_copy(ints.at[pl.ds(0, 8)], owner, sem)
    to_scalars.start()
    for k in range(n):
        count[k] = 0
    for k in range(n * cap):
        place[k] = 0
    table[...] = jnp.zeros_like(table)
    lists[...] = jnp.zeros_like(lists)

    distance = ints[0:1, :] ^ me
    as_column = jnp.sum(
        jnp.where(iota((rows, rows), 0) == iota((rows, rows), 1), distance, 0),
        axis=1,
        keepdims=True,
    )
    before = (as_column == distance) & (iota((rows, rows), 0) < iota((rows, rows), 1))
    rank = jnp.sum(before.astype(jnp.int32), axis=0, keepdims=True)
    odd = jnp.where(distance < 2, 0, distance % 2)
    place_of = (distance - odd) * LIST_ROWS + odd * 8 + rank
    chosen = iota((n * LIST_ROWS, rows), 0) == place_of
    table[0 : ints.shape[0], :] = ints[...].astype(F32)
    table[ints.shape[0] - pairs : ints.shape[0], :] += 1.0
    ordered = dot(chosen.astype(BF16), table[...].astype(BF16), (1, 1))
    lists[:, 0:128] = ordered.astype(BF16)

    to_scalars.wait()

    @pl.loop(0, rows, unroll=4)
    def _(e):
        k = owner[0, e] ^ me
        r = count[k]
        place[k * cap + r] = e
        count[k] = r + 1

    for k in range(n):
        for r in range(cap):
            outs[k][r * square : (r + 1) * square, :] = blocks[place[k * cap + r]]
        if list_height(k) > 0:
            outs[k][cap * square :, :] = lists[k * LIST_ROWS : (k + 1) * LIST_ROWS, :]


def pack(n, cap, blocks, block_owner, block_basis, pair_images, pair_cell):
    rows, square, width = blocks.shape
    pairs = pair_cell.shape[1]
    ints = jnp.concatenate(
        [
            block_owner.T,
            block_basis.T,
            jnp.transpose(pair_images, (1, 2, 0)).reshape(2 * pairs, rows),
            pair_cell.T,
        ],
        axis=0,
    )
    heights = [cap * square + list_height(k) for k in range(n)]
    return pl.pallas_call(
        functools.partial(pack_kernel, n, cap, pairs),
        out_shape=[jax.ShapeDtypeStruct((height, width), BF16) for height in heights],
        in_specs=[pl.BlockSpec(memory_space=pltpu.VMEM)] * 2,
        out_specs=[pl.BlockSpec(memory_space=pltpu.VMEM)] * n,
        scratch_shapes=[
            pltpu.SMEM((8, rows), jnp.int32),
            pltpu.VMEM((128, rows), F32),
            pltpu.VMEM((n * LIST_ROWS, width), BF16),
            pltpu.SMEM((n,), jnp.int32),
            pltpu.SMEM((n * cap,), jnp.int32),
            pltpu.SemaphoreType.DMA,
        ],
        compiler_params=pltpu.CompilerParams(vmem_limit_bytes=PACK_LIMIT),
        cost_estimate=pl.CostEstimate(flops=0, bytes_accessed=6 << 20, transcendentals=0),
        name="pack_by_owner",
    )(ints, blocks)


def by_halving(images):
    return images == 4


def row_parts(images, share):
    if by_halving(images):
        return [(0, DIRECT_ROWS), (DIRECT_ROWS, share - DIRECT_ROWS)]
    return [(0, share)]


def shares_of(images):
    if not by_halving(images):
        return [(0, [0], F32)] + [(0, [k], BF16) for k in range(1, images)]
    kept = [(0, [0], F32), (1, [0], F32), (1, [2], F32), (1, [1, 3], BF16)]
    return kept + [(0, [k], BF16) for k in (2, 3, 1)]


def diagonals(cap, pairs, cell_count, side, lists, table):
    images = lax.axis_size("image")
    z = lax.axis_index("image")
    square = side * side
    quad = min(QUAD, cap)
    lanes = quad * square
    height = 8 * len(lists)
    lane = iota((1, lanes), 1)
    listing = jnp.concatenate(
        [ref[at : at + LIST_ROWS, 0:128].astype(F32)[i : i + 8] for ref, at, i in lists], axis=0
    )

    def columns(start):
        return jnp.concatenate(
            [listing[:, start + j : start + j + 1] for j in range(pairs)], axis=0
        ).astype(jnp.int32)

    def side_by_side(rows, at):
        out = jnp.where(lane // square == 0, rows[at : at + 1], 0.0)
        for s in range(1, quad):
            out = jnp.where(lane // square == s, rows[at + s : at + s + 1], out)
        return out

    def density_rows(basis_at, image_at, lane_at):
        block = jnp.concatenate([listing[:, basis_at : basis_at + 1]] * pairs, axis=0)
        row = (columns(image_at) ^ z) * (table.shape[0] // images) + block.astype(jnp.int32)
        chosen = iota((height * pairs, table.shape[0]), 1) == row
        found = dot(jnp.where(chosen, 1.0, 0.0).astype(BF16), table[...])
        return jnp.concatenate([found[:, lane_at : lane_at + square]] * quad, axis=1)

    occ = density_rows(1, 3, 0)
    virt = density_rows(2, 3 + pairs, square)
    cell = jnp.broadcast_to(columns(3 + 2 * pairs).astype(F32), (height * pairs, lanes))

    shape = (square, lanes)
    occ_mask = (iota(shape, 1) % side == iota(shape, 0) // side).astype(BF16)
    virt_mask = (iota(shape, 1) % square // side == iota(shape, 0) % side).astype(BF16)
    shape = (lanes, lanes)
    occ_spread = (iota(shape, 0) // side == iota(shape, 1) // side).astype(BF16)
    virt_spread = (
        (iota(shape, 0) // square == iota(shape, 1) // square)
        & (iota(shape, 0) % side == iota(shape, 1) % side)
    ).astype(BF16)

    for p in range(len(lists)):
        for g in range(cap // quad):
            at = [j * height + 8 * p + g * quad for j in range(pairs)]
            occ_in = jnp.concatenate(
                [occ_mask * side_by_side(occ, a).astype(BF16) for a in at], axis=0
            )
            virt_in = jnp.concatenate(
                [virt_mask * side_by_side(virt, a).astype(BF16) for a in at], axis=0
            )
            terms = dot(occ_in, occ_spread) * dot(virt_in, virt_spread)
            here = [side_by_side(cell, a) for a in at]
            out = []
            for c in range(cell_count):
                op = None
                for j in range(pairs):
                    term = terms[j * square : (j + 1) * square]
                    term = jnp.where(here[j] == float(c + 1), term, 0.0)
                    op = term if op is None else op + term
                out.append(
                    jnp.concatenate(
                        [jnp.where(lane // square == s, op, 0.0) for s in range(quad)], axis=0
                    ).astype(BF16)
                )
            yield out


def early_kernel(count, cap, pairs, cell_count, square, first, *refs):
    refs = list(refs)
    images = lax.axis_size("image")
    payloads = [refs.pop(0) for _ in range(count)]
    if first:
        pieces = [refs.pop(0) for _ in range(images)]
        total, table, mixed, stacked = refs
        for i in range(images):
            block_count = pieces[i].shape[1]
            table[i * block_count : (i + 1) * block_count, :] = pieces[i][...].T
        before = None
    else:
        before, table, total, mixed, stacked = refs
    lists = [(p, cap * square, 0) for p in payloads]
    made = diagonals(cap, pairs, cell_count, math.isqrt(square), lists, table)
    add_blocks(cap, square, payloads, made, before, total, mixed, stacked)


def add_blocks(cap, square, payloads, made, before, total, mixed, stacked, kept=None):
    lanes = min(QUAD, cap) * square
    per = cap * square // lanes
    for i, operators in enumerate(made):
        p, g = divmod(i, per)
        block = payloads[p][g * lanes : (g + 1) * lanes, :]
        stacked[i * lanes : (i + 1) * lanes, :] = block
        turned = block.T
        if kept is not None:
            turned = jnp.concatenate([turned[rows] for rows in kept], axis=0)
        for c, operator in enumerate(operators):
            mixed[c, :, i * lanes : (i + 1) * lanes] = dot(turned, operator).astype(BF16)
    for c in range(mixed.shape[0]):
        acc = dot(mixed[c], stacked[...])
        if kept is not None:
            acc = acc + jnp.concatenate([before[c, rows, :] for rows in kept], axis=0)
        elif before is not None:
            acc = acc + before[c]
        total[c] = acc


def operators_kernel(count, cap, pairs, cell_count, square, lists, table, out):
    places = [(lists, i * LIST_ROWS, 8) for i in range(count)]
    made = diagonals(cap, pairs, cell_count, math.isqrt(square), places, table)
    for i, operators in enumerate(made):
        for c in range(cell_count):
            out[i * cell_count + c] = operators[c]


def late_kernel(count, cap, cell_count, square, part, *refs):
    refs = list(refs)
    images = lax.axis_size("image")
    payloads = [refs.pop(0) for _ in range(count)]
    before, operators = refs.pop(0), refs.pop(0)
    made = (
        [operators[i * cell_count + c] for c in range(cell_count)]
        for i in range(operators.shape[0] // cell_count)
    )
    if part is None:
        total, mixed, stacked = refs
        add_blocks(cap, square, payloads, made, before, total, mixed, stacked)
        return
    share = before.shape[1] // images
    start, rows = row_parts(images, share)[part]
    held = [entry for entry in shares_of(images) if entry[0] == part]
    outs = [refs.pop(0) for _ in held]
    total, mixed, stacked = refs
    kept = [slice(i * share + start, i * share + start + rows) for i in range(images)]
    add_blocks(cap, square, payloads, made, before, total, mixed, stacked, kept)
    z = lax.axis_index("image")
    for ref, (_, distances, _) in zip(outs, held):
        for i, k in enumerate(distances):
            at = pl.multiple_of((z ^ k) * rows, 16)
            taken = total[:, pl.ds(at, rows), :].astype(ref.dtype)
            ref[i * cell_count : (i + 1) * cell_count] = taken


def on_chip(kernel, name, args, out_shape, scratch=()):
    vmem = pl.BlockSpec(memory_space=pltpu.VMEM)
    return pl.pallas_call(
        kernel,
        out_shape=out_shape,
        in_specs=[vmem] * len(args),
        out_specs=[vmem] * len(out_shape),
        scratch_shapes=list(scratch),
        compiler_params=pltpu.CompilerParams(vmem_limit_bytes=VMEM_LIMIT),
        cost_estimate=pl.CostEstimate(
            flops=CHI_FLOPS, bytes_accessed=CHI_BYTES, transcendentals=0
        ),
        name=name,
    )(*args)


def chi_scratch(cell_count, width, depth):
    return [pltpu.VMEM((cell_count, width, depth), BF16), pltpu.VMEM((depth, width), BF16)]


def early_part(cap, pairs, cell_count, square, payloads, given, first):
    count, width = len(payloads), payloads[0].shape[1]
    out_shape = [jax.ShapeDtypeStruct((cell_count, width, width), F32)]
    if first:
        shape = (len(given) * given[0].shape[1], given[0].shape[0])
        out_shape.append(jax.ShapeDtypeStruct(shape, BF16))
    return on_chip(
        functools.partial(early_kernel, count, cap, pairs, cell_count, square, first),
        "chi_of_early_payloads",
        list(payloads) + list(given),
        out_shape,
        chi_scratch(cell_count, width, count * cap * square),
    )


def operators_part(cap, pairs, cell_count, square, lists, table):
    count = lists.shape[0] // LIST_ROWS
    lanes = min(QUAD, cap) * square
    groups = count * cap * square // lanes
    return on_chip(
        functools.partial(operators_kernel, count, cap, pairs, cell_count, square),
        "operators_of_late_payloads",
        [lists, table],
        [jax.ShapeDtypeStruct((groups * cell_count, lanes, lanes), BF16)],
    )[0]


def late_part(cap, cell_count, square, images, payloads, before, operators, part):
    count, width = len(payloads), payloads[0].shape[1]
    depth = count * cap * square
    scratch = chi_scratch(cell_count, width, depth)
    out_shape = [jax.ShapeDtypeStruct((cell_count, width, width), F32)]
    if part is not None:
        rows = row_parts(images, width // images)[part][1]
        out_shape = [
            jax.ShapeDtypeStruct((len(distances) * cell_count, rows, width), dtype)
            for of, distances, dtype in shares_of(images)
            if of == part
        ]
        scratch = [pltpu.VMEM((cell_count, images * rows, width), F32)] + chi_scratch(
            cell_count, images * rows, depth
        )
        scratch[2] = pltpu.VMEM((depth, width), BF16)
    return on_chip(
        functools.partial(late_kernel, count, cap, cell_count, square, part),
        "chi_of_late_payloads",
        list(payloads) + [before, operators],
        out_shape,
        scratch,
    )


def transform_kernel(cell_count, step, row_at, phases, own, *rest):
    *received, out, total, shaped, sems = rest
    acc = own[...]
    for part in received:
        acc = acc + part[0:cell_count].astype(F32)
    total[...] = acc
    points, rows, width = shaped.shape

    def copy(i):
        at = pl.ds(i * step, step)
        return pltpu.make_async_copy(
            shaped.at[at], out.at[at, pl.ds(row_at, rows)], sems.at[i]
        )

    @pl.loop(0, points // step)
    def _(i):
        parts = [total[c] for c in range(cell_count)]
        for j in range(step):
            acc = phases[0, i * step + j] * parts[0]
            for c in range(1, cell_count):
                acc = acc + phases[c, i * step + j] * parts[c]
            shaped[i * step + j] = acc
        copy(i).start()

    @pl.loop(0, points // step)
    def _(i):
        copy(i).wait()


def transform(phases, own, received, row_at, share, so_far):
    cell_count, rows, width = own.shape
    points = phases.shape[1]
    step = 16
    vmem = pl.BlockSpec(memory_space=pltpu.VMEM)
    hbm = pl.BlockSpec(memory_space=pltpu.HBM)
    args = [phases, own, *received]
    specs = [pl.BlockSpec(memory_space=pltpu.SMEM)] + [vmem] * (1 + len(received))
    aliases = {}
    kernel = functools.partial(transform_kernel, cell_count, step, row_at)
    if so_far is not None:
        aliases = {len(args): 0}
        inner = kernel
        at = len(args)

        def kernel(*refs):
            inner(*refs[:at], *refs[at + 1 :])

        args.append(so_far)
        specs.append(hbm)
    return pl.pallas_call(
        kernel,
        out_shape=jax.ShapeDtypeStruct((points, share, width), F32),
        in_specs=specs,
        out_specs=hbm,
        input_output_aliases=aliases,
        scratch_shapes=[
            pltpu.VMEM((cell_count, rows, width), F32),
            pltpu.VMEM((points, rows, width), F32),
            pltpu.SemaphoreType.DMA((points // step,)),
        ],
        compiler_params=pltpu.CompilerParams(vmem_limit_bytes=VMEM_LIMIT),
        cost_estimate=pl.CostEstimate(
            flops=2 * points * cell_count * rows * width,
            bytes_accessed=points * rows * width * 4,
            transcendentals=0,
        ),
        name="to_k_points",
    )(*args)


def swap(array, axis, k):
    size = lax.axis_size(axis)
    return lax.ppermute(array, axis, [(i, i ^ k) for i in range(size)])


def local(blocks, block_owner, block_basis, pair_images, pair_cell, lattice, dens_occ, dens_virt):
    owners, images = lax.axis_size("ri"), lax.axis_size("image")
    pairs = pair_cell.shape[1]
    cell_count = lattice.shape[0]
    cap = max(2, (2 * blocks.shape[0] + owners - 1) // owners)

    packed = pack(owners, cap, blocks, block_owner, block_basis, pair_images, pair_cell)
    square = blocks.shape[1]
    evens = [6, 2, 4] if owners == 8 else list(range(owners - 2, 1, -2))
    odds = [k ^ 1 for k in evens]
    payload = {0: packed[0]}
    payload.update({k: swap(packed[k], "ri", k) for k in evens})
    for k in odds:
        payload[k ^ 1], later = lax.optimization_barrier((payload[k ^ 1], packed[k]))
        payload[k] = swap(later, "ri", k)
    payload[1], dens_occ, dens_virt = lax.optimization_barrier(
        (swap(packed[1], "ri", 1), dens_occ, dens_virt)
    )
    lists = [payload[k][cap * square :] for k in evens]
    lists = swap(jnp.concatenate(lists, axis=0), "ri", 1)
    density = jnp.concatenate([dens_occ[0].T, dens_virt[0].T], axis=0)
    pieces = density[None]
    k = 1
    while k < images:
        pieces = jnp.concatenate([pieces, swap(pieces, "image", k)], axis=0)
        k = 2 * k
    pieces = [pieces[i] for i in range(images)]

    given = pieces
    early = [0, 1] + evens
    for at in range(0, len(early), PART):
        chosen = [payload[k] for k in early[at : at + PART]]
        out = early_part(cap, pairs, cell_count, square, chosen, given, at == 0)
        table = out[1] if at == 0 else table
        given = [out[0], table]
    chi = out[0]
    for at in range(0, len(odds), PART):
        chosen = [payload[k] for k in odds[at : at + PART]]
        part = lists[at * LIST_ROWS : (at + len(chosen)) * LIST_ROWS]
        operators = operators_part(cap, pairs, cell_count, square, part, table)
        args = (cap, cell_count, square, images, chosen, chi, operators)
        if at + PART < len(odds):
            chi = late_part(*args, None)[0]
            continue
        count = len(row_parts(images, blocks.shape[2] // images))
        by_part = {part: iter(late_part(*args, part)) for part in reversed(range(count))}
        out = [next(by_part[part]) for part, _, _ in shares_of(images)]
    plan = shares_of(images)
    parts = [[x] for x, (_, distances, _) in zip(out, plan) if distances == [0]]
    given = dict(zip([(part, distances[0]) for part, distances, _ in plan], out))
    for part, distances, dtype in plan:
        if dtype == BF16:
            k = distances[0]
            parts[part].append(swap(given[part, k], "image", k))
    if by_halving(images):
        forward = parts[1][1][cell_count:].astype(F32) + given[1, 2]
        parts[1].append(swap(forward.astype(BF16), "image", 2))

    points = jnp.arange(KGRID * KGRID, dtype=jnp.int32)
    wrapped = (
        lattice[:, 0:1] * (points // KGRID)[None, :] + lattice[:, 1:2] * (points % KGRID)[None, :]
    ) % KGRID
    angles = 2.0 * math.pi / KGRID * wrapped.astype(F32)
    phases = jnp.concatenate([jnp.cos(angles), jnp.sin(angles)], axis=1)
    result = None
    share = blocks.shape[2] // images
    places = list(zip(row_parts(images, share), parts))
    for (row_at, _), (own, *received) in places:
        result = transform(phases, own, received, row_at, share, result)
    return result.reshape((2, KGRID * KGRID, 1) + result.shape[1:])


def solution(mesh):
    placed = (
        P(("image", "ri"), None, None),
        P(("image", "ri"), None),
        P(("image", "ri"), None),
        P(("image", "ri"), None, None),
        P(("image", "ri"), None),
        P(),
        P("image", None, None),
        P("image", None, None),
    )
    return jax.shard_map(
        local,
        mesh=mesh,
        in_specs=placed,
        out_specs=P(None, None, "ri", "image", None),
        check_vma=False,
    )
```
